256 devices in a mesh: batch: 8 (over x, core), branch: 32 (over z, y).
Axes of the slice: x: 4, y: 4, z: 8, core: 2. Of those that a mesh axis runs over, the one named last changes fastest.
Arguments:
- queries: bfloat16 [256, 128, 16, 128], P(('batch', 'branch')), parts along dimension 0, may hold values from -6 to 6
- response_keys: bfloat16 [256, 128, 4, 128], P(('batch', 'branch')), parts along dimension 0, may hold values from -6 to 6
- response_values: bfloat16 [256, 128, 4, 128], P(('batch', 'branch')), parts along dimension 0, may hold values from -6 to 6
- prompt_keys: bfloat16 [16384, 4, 128], P(('batch', 'branch')), parts along dimension 0, may hold values from -6 to 6
- prompt_value_rows: bfloat16 [16384, 4, 128], P(('batch', 'branch')), parts along dimension 0, may hold values from -6 to 6
- lengths: int32 [256], P(('batch', 'branch')), parts along dimension 0, may hold values from 16 to 128, as said below
- grad_out: bfloat16 [256, 128, 16, 128], P(('batch', 'branch')), parts along dimension 0, may hold values from -6 to 6
Outputs:
- attended: bfloat16 [256, 128, 16, 128], P(('batch', 'branch')), parts along dimension 0
- grad_query: bfloat16 [256, 128, 16, 128], P(('batch', 'branch')), parts along dimension 0
- grad_resp_keys: bfloat16 [256, 128, 4, 128], P(('batch', 'branch')), parts along dimension 0
- grad_resp_values: bfloat16 [256, 128, 4, 128], P(('batch', 'branch')), parts along dimension 0
- grad_prompt_keys: bfloat16 [16384, 4, 128], P(('batch', 'branch')), parts along dimension 0
- grad_prompt_values: bfloat16 [16384, 4, 128], P(('batch', 'branch')), parts along dimension 0
The draws below stay inside these ranges and needn't reach their ends.
There are 8 independent parts, one for each index of `batch`. The reference program is written for one: setup_inputs(seed, part) draws one part's arguments, and reference() takes and returns one part's arrays. A program takes and returns all parts, laid end to end along the dimension named above; each array names one. Nothing has to cross between parts.
Inputs may be any that keep to these rules, and one draw needn't show every extreme that they name: `lengths`: some response of every prompt has all 128 slots live.
All inputs are finite; a program needn't handle non-finite values.
Results may differ from the reference program's by a relative error of at most 0.034.
Values may be sent and summed in bfloat16 or wider, within the bound.
No kernel may reach another device: no remote copies, remote signals or barrier semaphores. Data moves between devices by JAX's collectives and lax.ppermute only.
A program may use at most 192 MiB of HBM per device.

```python
import jax
import jax.numpy as jnp
from jax import lax

HQ = 16
KEY_VALUE_HEADS = 4
HEAD_SIZE = 128
PROMPT_TOKENS = 2048
RESPONSE_LENGTH = 128
RESPONSE_COUNT = 32


def draw_queries(key, part):
    key = jax.random.fold_in(key, 1)
    tensor_dims = (RESPONSE_COUNT, RESPONSE_LENGTH, HQ, HEAD_SIZE)
    drawn_vals = jnp.clip(jax.random.normal(key, tensor_dims, jnp.float32), -6.0, 6.0)
    return drawn_vals.astype(jnp.bfloat16)


def draw_prompt_keys(key, part):
    key = jax.random.fold_in(key, 2)
    tensor_dims = (PROMPT_TOKENS, KEY_VALUE_HEADS, HEAD_SIZE)
    drawn_vals = jnp.clip(jax.random.normal(key, tensor_dims, jnp.float32), -6.0, 6.0)
    return drawn_vals.astype(jnp.bfloat16)


def draw_lengths(key, part):
    key = jax.random.fold_in(key, 5)
    shortest = max(1, RESPONSE_LENGTH // 8)
    drawn_vals = jax.random.randint(key, (RESPONSE_COUNT,), shortest, RESPONSE_LENGTH + 1)
    longest = jax.random.randint(jax.random.fold_in(key, 6), (), 0, RESPONSE_COUNT)
    return jnp.where(jnp.arange(RESPONSE_COUNT) == longest, RESPONSE_LENGTH, drawn_vals).astype(jnp.int32)


def level_of(rng, shape, cuts, smallest, high):
    def one(dim, parts):
        heights = jax.random.uniform(jax.random.fold_in(jax.random.fold_in(rng, 6), dim), (parts,), jnp.float32, smallest / len(cuts), high / len(cuts))
        return jnp.repeat(jnp.exp(heights), shape[dim] // parts).reshape((-1,) + (1,) * (len(shape) - dim - 1))

    factor_of = one(*cuts[0])
    for cut in cuts[1:]:
        factor_of = factor_of * one(*cut)
    return factor_of


def bell_draw(key, dims, spread, reach, pieces=(), held_as=jnp.bfloat16):
    drawn = jax.random.normal(key, dims, jnp.float32) * spread
    if len(pieces) > 0:
        drawn = level_of(key, dims, pieces, -0.22, 0.18) * drawn
    return jnp.clip(drawn, min=-reach, max=reach).astype(held_as)


def setup_inputs(seed: int = 0, part: int = 0) -> dict:
    seeds = jax.random.split(jax.random.key(seed), 8)
    part_keys = jax.random.split(jax.random.fold_in(seeds[7], part), 8)
    return {
        "queries": draw_queries(jax.random.fold_in(jax.random.fold_in(seeds[7], part), 71), part),
        "response_keys": bell_draw(part_keys[1], (RESPONSE_COUNT, RESPONSE_LENGTH, KEY_VALUE_HEADS, HEAD_SIZE), 1.0, 6.0, ((0, 32),)),
        "response_values": bell_draw(part_keys[2], (RESPONSE_COUNT, RESPONSE_LENGTH, KEY_VALUE_HEADS, HEAD_SIZE), 1.0, 6.0, ((0, 32),)),
        "prompt_keys": draw_prompt_keys(jax.random.fold_in(jax.random.fold_in(seeds[7], part), 71), part),
        "prompt_value_rows": bell_draw(part_keys[4], (PROMPT_TOKENS, KEY_VALUE_HEADS, HEAD_SIZE), 1.0, 6.0, ((0, 32),)),
        "lengths": draw_lengths(jax.random.fold_in(jax.random.fold_in(seeds[7], part), 71), part),
        "grad_out": bell_draw(part_keys[6], (RESPONSE_COUNT, RESPONSE_LENGTH, HQ, HEAD_SIZE), 1.0, 6.0, ((0, 32),)),
    }


masked_score = -1.0e30


def one_response(query_rows, resp_key, resp_value, prompt_key, prompt_value, length, grad_rows):
    seq_len, num_heads, head_dim = query_rows.shape
    kv_heads = prompt_key.shape[1]
    group_size = num_heads // kv_heads
    prompt_len = prompt_key.shape[0]
    score_scale = head_dim ** -0.5
    keys_all = jnp.concatenate([prompt_key, resp_key], axis=0).astype(jnp.float32)
    values_all = jnp.concatenate([prompt_value, resp_value], axis=0).astype(jnp.float32)
    grouped = query_rows.reshape(seq_len, kv_heads, group_size, head_dim).astype(jnp.float32)
    row_ids = jnp.arange(seq_len)
    col_ids = jnp.arange(prompt_len + seq_len)
    allowed = (col_ids[None, :] < prompt_len) | (col_ids[None, :] - prompt_len <= row_ids[:, None])
    live_rows = (row_ids < length)[:, None, None, None]
    scores = jnp.einsum("tkgd,skd->kgts", grouped, keys_all) * score_scale
    scores = jnp.where(allowed, scores, masked_score)
    top_score = jnp.max(scores, axis=-1, keepdims=True)
    log_total = top_score + jnp.log(jnp.sum(jnp.exp(scores - top_score), axis=-1, keepdims=True))
    weights = jnp.exp(scores - log_total)
    weights_low = lax.optimization_barrier(weights.astype(jnp.bfloat16)).astype(jnp.float32)
    attended = jnp.einsum("kgts,skd->tkgd", weights_low, values_all)
    attended = jnp.where(live_rows, attended, 0.0).astype(jnp.bfloat16)
    masked = jnp.where(live_rows, grad_rows.reshape(seq_len, kv_heads, group_size, head_dim).astype(jnp.float32), 0.0)
    row_delta = jnp.sum(masked * attended.astype(jnp.float32), axis=-1)
    dweights = jnp.einsum("tkgd,skd->kgts", masked, values_all)
    dscores = weights * (dweights - jnp.transpose(row_delta, (1, 2, 0))[..., None])
    dscores = lax.optimization_barrier(dscores.astype(jnp.bfloat16)).astype(jnp.float32)
    grad_query = (jnp.einsum("kgts,skd->tkgd", dscores, keys_all) * score_scale).astype(jnp.bfloat16)
    grad_keys = jnp.einsum("kgts,tkgd->skd", dscores, grouped) * score_scale
    grad_values = jnp.einsum("kgts,tkgd->skd", weights_low, masked)
    return (attended.reshape(seq_len, num_heads, head_dim),
            grad_query.reshape(seq_len, num_heads, head_dim),
            grad_keys[prompt_len:].astype(jnp.bfloat16),
            grad_values[prompt_len:].astype(jnp.bfloat16),
            grad_keys[:prompt_len],
            grad_values[:prompt_len])


def reference(queries, response_keys, response_values, prompt_keys, prompt_value_rows, lengths, grad_out):
    def step_one(members):
        return one_response(members[0], members[1], members[2], prompt_keys, prompt_value_rows, members[3], members[4])

    attended, grad_query, grad_rk, grad_rv, prompt_dk, prompt_dv = lax.map(
        step_one, (queries, response_keys, response_values, lengths, grad_out))
    return (attended, grad_query, grad_rk, grad_rv,
            jnp.sum(prompt_dk, axis=0).astype(jnp.bfloat16),
            jnp.sum(prompt_dv, axis=0).astype(jnp.bfloat16))
```

```python
import jax
import jax.numpy as jnp
from jax import lax
from jax.experimental import pallas as pl
from jax.experimental.pallas import tpu as pltpu
from jax.sharding import Mesh, PartitionSpec as P

LOG2E = 1.4426950408889634
CHUNK = 512
f32 = jnp.float32
bf16 = jnp.bfloat16
NT = (((1,), (1,)), ((), ()))
NN = (((1,), (0,)), ((), ()))


def dot(a, b, dims):
    return lax.dot_general(a, b, dims, preferred_element_type=f32)


def attention_kernel(
    *refs, rows_per, own_len, head_dim, group, spots,
):
    n_in = 4 + 9
    packs = refs[0:4]
    kvs = refs[4:13]
    out_packs = refs[13:17]
    out_kvs = refs[17:26]
    K, V, S, Pm, KT, VT, Qn, On, stat, dqt = refs[26:]
    R = rows_per
    T = own_len
    D = head_dim
    C = D ** (-0.5)
    nk = spots * 8
    nch = nk // CHUNK
    for i in range(7):
        K[i * spots:(i + 1) * spots, :] = kvs[i][0]
        V[i * spots:(i + 1) * spots, :] = kvs[i][1]
    K[7 * spots:8 * spots, :] = kvs[7][...]
    V[7 * spots:8 * spots, :] = kvs[8][...]
    for c in range(nch):
        KT[:, c * CHUNK:(c + 1) * CHUNK] = K[c * CHUNK:(c + 1) * CHUNK, :].T
        VT[0:D, c * CHUNK:(c + 1) * CHUNK] = V[c * CHUNK:(c + 1) * CHUNK, :].T
    VT[D:D + 16, :] = jnp.ones((16, nk), bf16)
    key_pos = lax.broadcasted_iota(jnp.int32, (T, R), 0)
    row_pos = lax.broadcasted_iota(jnp.int32, (T, R), 1) // group
    for r in range(4):
        rows = slice(r * R, (r + 1) * R)
        qr = packs[r][0:R, :]
        dor = packs[r][R:2 * R, :]
        kr = packs[r][2 * R:2 * R + T, :]
        vr = packs[r][2 * R + T:2 * R + 2 * T, :]
        top = jnp.full((8, R), -jnp.inf, f32)
        for c in range(nch):
            s = dot(K[c * CHUNK:(c + 1) * CHUNK, :], qr, NT)
            S[c * CHUNK:(c + 1) * CHUNK, :] = s
            top = jnp.maximum(top, jnp.max(s.reshape(CHUNK // 8, 8, R), axis=0))
        s = dot(kr, qr, NT)
        s = jnp.where(key_pos <= row_pos, s, -1e30)
        S[nk:nk + T, :] = s
        top = jnp.maximum(top, jnp.max(s.reshape(T // 8, 8, R), axis=0))
        top = jnp.max(top, axis=0, keepdims=True) * (C * LOG2E)
        acc = jnp.zeros((D + 16, R), f32)
        for c in range(nch):
            p = jnp.exp2(S[c * CHUNK:(c + 1) * CHUNK, :] * (C * LOG2E) - top).astype(bf16)
            Pm[c * CHUNK:(c + 1) * CHUNK, rows] = p
            acc = acc + dot(VT[:, c * CHUNK:(c + 1) * CHUNK], p, NN)
        p = jnp.exp2(S[nk:nk + T, :] * (C * LOG2E) - top).astype(bf16)
        Pm[nk:nk + T, rows] = p
        acc = acc + dot(jnp.concatenate([vr.T, jnp.ones((16, T), bf16)], axis=0), p, NN)
        inv = 1.0 / acc[D:D + 1, :]
        o = (acc[0:D, :] * inv).T.astype(bf16)
        out_packs[r][0:R, :] = o
        dof = dor.astype(f32)
        delta = jnp.sum(dof * o.astype(f32), axis=1, keepdims=True)
        stat[0:1, rows] = jnp.broadcast_to(delta, (R, D)).T[0:1, :]
        stat[1:2, rows] = inv
        inv_col = jnp.broadcast_to(inv, (D, R)).T
        Qn[rows, :] = (qr.astype(f32) * (inv_col * C)).astype(bf16)
        On[rows, :] = (dof * inv_col).astype(bf16)
    for r in range(4):
        rows = slice(r * R, (r + 1) * R)
        dor = packs[r][R:2 * R, :]
        kr = packs[r][2 * R:2 * R + T, :]
        vr = packs[r][2 * R + T:2 * R + 2 * T, :]
        p = Pm[nk:nk + T, rows]
        ds = (p.astype(f32) * (dot(vr, dor, NT) - stat[0:1, rows])).astype(bf16)
        out_packs[r][2 * R:2 * R + T, :] = dot(ds, Qn[rows, :], NN).astype(bf16)
        out_packs[r][2 * R + T:2 * R + 2 * T, :] = dot(p, On[rows, :], NN).astype(bf16)
        dqt[:, rows] = dot(kr.T, ds, NN)
    for c in range(nch):
        ks = slice(c * CHUNK, (c + 1) * CHUNK)
        dk = jnp.zeros((CHUNK, D), f32)
        dv = jnp.zeros((CHUNK, D), f32)
        for r in range(4):
            rows = slice(r * R, (r + 1) * R)
            p = Pm[ks, rows]
            dp = dot(V[ks, :], packs[r][R:2 * R, :], NT)
            ds = (p.astype(f32) * (dp - stat[0:1, rows])).astype(bf16)
            dk = dk + dot(ds, Qn[rows, :], NN)
            dv = dv + dot(p, On[rows, :], NN)
            dqt[:, rows] += dot(KT[:, ks], ds, NN)
        for j in range(CHUNK // spots):
            i = c * (CHUNK // spots) + j
            part = slice(j * spots, (j + 1) * spots)
            if i < 7:
                out_kvs[i][0] = dk[part, :].astype(bf16)
                out_kvs[i][1] = dv[part, :].astype(bf16)
            else:
                out_kvs[7][...] = dk[part, :].astype(bf16)
                out_kvs[8][...] = dv[part, :].astype(bf16)
    for r in range(4):
        rows = slice(r * R, (r + 1) * R)
        out_packs[r][R:2 * R, :] = (dqt[:, rows] * (stat[1:2, rows] * C)).T.astype(bf16)


def attention_call(packs, kvs, rows_per, own_len, head_dim, group):
    spots = kvs[0].shape[1]
    nk = spots * 8
    shapes = [jax.ShapeDtypeStruct(x.shape, bf16) for x in list(packs) + list(kvs)]
    rows = 4 * rows_per

    def body(*refs):
        attention_kernel(
            *refs, rows_per=rows_per, own_len=own_len, head_dim=head_dim, group=group, spots=spots
        )

    outs = pl.pallas_call(
        body,
        out_shape=shapes,
        scratch_shapes=[
            pltpu.VMEM((nk, head_dim), bf16),
            pltpu.VMEM((nk, head_dim), bf16),
            pltpu.VMEM((nk + own_len, rows_per), f32),
            pltpu.VMEM((nk + own_len, rows), bf16),
            pltpu.VMEM((head_dim, nk), bf16),
            pltpu.VMEM((head_dim + 16, nk), bf16),
            pltpu.VMEM((rows, head_dim), bf16),
            pltpu.VMEM((rows, head_dim), bf16),
            pltpu.VMEM((8, rows), f32),
            pltpu.VMEM((head_dim, rows), f32),
        ],
        compiler_params=pltpu.CompilerParams(vmem_limit_bytes=56 * 2**20),
        name="attention",
    )(*packs, *kvs)
    return outs[0:4], outs[4:]


def on_device(
    queries, response_keys, response_values, prompt_keys, prompt_value_rows, lengths, grad_out
):
    _, T, H, D = queries.shape
    KH = prompt_keys.shape[1]
    G = H // KH
    R = T * G
    spots = prompt_keys.shape[0]
    my_y = lax.axis_index("y")

    def over_z(x, k):
        return lax.ppermute(x, "z", [(i, (i + k) % 8) for i in range(8)])

    def over_y(x, k):
        return lax.ppermute(x, "y", [(i, (i + k) % 4) for i in range(4)])

    def head_of(k):
        return (my_y + k) % KH

    kv = jnp.stack([prompt_keys, prompt_value_rows], axis=0)
    kv = jnp.transpose(kv, (2, 0, 1, 3))
    kv = lax.all_to_all(kv, "y", 0, 0, tiled=True)
    kv = jnp.transpose(kv, (1, 0, 2, 3)).reshape(2, 4 * spots, D)
    from_1 = over_z(kv, 1)
    from_m1 = over_z(kv, -1)
    from_2 = over_z(kv, 2)
    from_m2 = over_z(kv, -2)
    from_3 = over_z(from_2, 1)
    from_m3 = over_z(from_m2, -1)
    from_4k = over_z(from_2[0], 2)
    from_4v = over_z(from_m2[1], -2)

    live = (jnp.arange(T) < lengths[0])[:, None, None]
    masked = jnp.where(live, grad_out[0], jnp.zeros((), bf16))

    def pack(k):
        h = head_of(k)
        return jnp.concatenate(
            [
                lax.dynamic_slice_in_dim(queries[0], h * G, G, 1).reshape(R, D),
                lax.dynamic_slice_in_dim(masked, h * G, G, 1).reshape(R, D),
                lax.dynamic_slice_in_dim(response_keys[0], h, 1, 1).reshape(T, D),
                lax.dynamic_slice_in_dim(response_values[0], h, 1, 1).reshape(T, D),
            ],
            axis=0,
        )

    shifts = (0, 1, -1, 2)
    packs = [pack(k) if k == 0 else over_y(pack(k), k) for k in shifts]

    kvs = [kv, from_1, from_m1, from_2, from_m2, from_3, from_m3, from_4k, from_4v]
    outs, dkv = attention_call(packs, kvs, R, T, D, G)

    d0, d1, dm1, d2, dm2, d3, dm3, d4k, d4v = dkv
    via_1 = over_z(d3, -1)
    via_m1 = over_z(dm3, 1)
    via_2 = over_z(d4k, -2)
    via_m2 = over_z(d4v, 2)
    far_k = (d2[0].astype(f32) + via_1[0].astype(f32) + via_2.astype(f32)).astype(bf16)
    far_v = (d2[1].astype(f32) + via_1[1].astype(f32)).astype(bf16)
    far_mk = (dm2[0].astype(f32) + via_m1[0].astype(f32)).astype(bf16)
    far_mv = (dm2[1].astype(f32) + via_m1[1].astype(f32) + via_m2.astype(f32)).astype(bf16)
    parts = [
        over_z(d1, -1),
        over_z(dm1, 1),
        over_z(jnp.stack([far_k, far_v]), -2),
        over_z(jnp.stack([far_mk, far_mv]), 2),
    ]
    total = d0.astype(f32)
    for x in parts:
        total = total + x.astype(f32)
    total = jnp.transpose(total.astype(bf16).reshape(2, 4, spots, D), (1, 0, 2, 3))
    total = lax.all_to_all(total, "y", 0, 0, tiled=True)
    total = jnp.transpose(total, (1, 2, 0, 3))

    home = [outs[i] if k == 0 else over_y(outs[i], -k) for i, k in enumerate(shifts)]
    attended = jnp.zeros((T, H, D), bf16)
    grad_query = jnp.zeros((T, H, D), bf16)
    grad_rk = jnp.zeros((T, KH, D), bf16)
    grad_rv = jnp.zeros((T, KH, D), bf16)
    for x, k in zip(home, shifts):
        h = head_of(k)
        attended = lax.dynamic_update_slice_in_dim(attended, x[0:R].reshape(T, G, D), h * G, 1)
        grad_query = lax.dynamic_update_slice_in_dim(
            grad_query, x[R:2 * R].reshape(T, G, D), h * G, 1
        )
        grad_rk = lax.dynamic_update_slice_in_dim(
            grad_rk, x[2 * R:2 * R + T].reshape(T, 1, D), h, 1
        )
        grad_rv = lax.dynamic_update_slice_in_dim(
            grad_rv, x[2 * R + T:2 * R + 2 * T].reshape(T, 1, D), h, 1
        )
    attended = jnp.where(live, attended, jnp.zeros((), bf16))
    return (
        attended[None],
        grad_query[None],
        grad_rk[None],
        grad_rv[None],
        total[0],
        total[1],
    )


def solution(mesh):
    split = Mesh(mesh.devices.reshape(8, 8, 4), ("batch", "z", "y"))
    spec = P(("batch", "z", "y"))
    return jax.shard_map(
        on_device,
        mesh=split,
        in_specs=(spec,) * 7,
        out_specs=(spec,) * 6,
        check_vma=False,
    )
```

```python
import jax
import jax.numpy as jnp
from jax import lax
from jax.experimental import pallas as pl
from jax.experimental.pallas import tpu as pltpu
from jax.sharding import Mesh, PartitionSpec as P

LOG2E = 1.4426950408889634
CHUNK = 512
f32 = jnp.float32
bf16 = jnp.bfloat16
NT = (((1,), (1,)), ((), ()))
NN = (((1,), (0,)), ((), ()))


def dot(a, b, dims):
    return lax.dot_general(a, b, dims, preferred_element_type=f32)


def attention_kernel(*refs, rows_per, own_len, head_dim, group, spots):
    pack = refs[0]
    kvs = refs[1:9]
    out_pack = refs[9]
    out_kvs = refs[10:18]
    K, V, S, Pm, KT, VT, Qn, On, stat, dqt = refs[18:]
    R = rows_per
    T = own_len
    D = head_dim
    C = D ** (-0.5)
    nk = K.shape[0]
    nch = nk // CHUNK
    for i in range(8):
        for j in range(4):
            at = (4 * i + j) * spots
            K[at:at + spots, :] = kvs[i][j, 0]
            V[at:at + spots, :] = kvs[i][j, 1]
    for c in range(nch):
        KT[:, c * CHUNK:(c + 1) * CHUNK] = K[c * CHUNK:(c + 1) * CHUNK, :].T
        VT[0:D, c * CHUNK:(c + 1) * CHUNK] = V[c * CHUNK:(c + 1) * CHUNK, :].T
    VT[D:D + 16, :] = jnp.ones((16, nk), bf16)
    key_pos = lax.broadcasted_iota(jnp.int32, (T, R), 0)
    row_pos = lax.broadcasted_iota(jnp.int32, (T, R), 1) // group
    for r in range(4):
        rows = slice(r * R, (r + 1) * R)
        qr = pack[r, 0:R, :]
        dor = pack[r, R:2 * R, :]
        kr = pack[r, 2 * R:2 * R + T, :]
        vr = pack[r, 2 * R + T:2 * R + 2 * T, :]
        top = jnp.full((8, R), -jnp.inf, f32)
        for c in range(nch):
            s = dot(K[c * CHUNK:(c + 1) * CHUNK, :], qr, NT)
            S[c * CHUNK:(c + 1) * CHUNK, :] = s
            top = jnp.maximum(top, jnp.max(s.reshape(CHUNK // 8, 8, R), axis=0))
        s = dot(kr, qr, NT)
        s = jnp.where(key_pos <= row_pos, s, -1e30)
        S[nk:nk + T, :] = s
        top = jnp.maximum(top, jnp.max(s.reshape(T // 8, 8, R), axis=0))
        top = jnp.max(top, axis=0, keepdims=True) * (C * LOG2E)
        acc = jnp.zeros((D + 16, R), f32)
        for c in range(nch):
            p = jnp.exp2(S[c * CHUNK:(c + 1) * CHUNK, :] * (C * LOG2E) - top).astype(bf16)
            Pm[c * CHUNK:(c + 1) * CHUNK, rows] = p
            acc = acc + dot(VT[:, c * CHUNK:(c + 1) * CHUNK], p, NN)
        p = jnp.exp2(S[nk:nk + T, :] * (C * LOG2E) - top).astype(bf16)
        Pm[nk:nk + T, rows] = p
        acc = acc + dot(jnp.concatenate([vr.T, jnp.ones((16, T), bf16)], axis=0), p, NN)
        inv = 1.0 / acc[D:D + 1, :]
        o = (acc[0:D, :] * inv).T.astype(bf16)
        out_pack[r, 0:R, :] = o
        dof = dor.astype(f32)
        delta = jnp.sum(dof * o.astype(f32), axis=1, keepdims=True)
        stat[0:1, rows] = jnp.broadcast_to(delta, (R, D)).T[0:1, :]
        stat[1:2, rows] = inv
        inv_col = jnp.broadcast_to(inv, (D, R)).T
        Qn[rows, :] = (qr.astype(f32) * (inv_col * C)).astype(bf16)
        On[rows, :] = (dof * inv_col).astype(bf16)
    for r in range(4):
        rows = slice(r * R, (r + 1) * R)
        dor = pack[r, R:2 * R, :]
        kr = pack[r, 2 * R:2 * R + T, :]
        vr = pack[r, 2 * R + T:2 * R + 2 * T, :]
        p = Pm[nk:nk + T, rows]
        ds = (p.astype(f32) * (dot(vr, dor, NT) - stat[0:1, rows])).astype(bf16)
        out_pack[r, 2 * R:2 * R + T, :] = dot(ds, Qn[rows, :], NN).astype(bf16)
        out_pack[r, 2 * R + T:2 * R + 2 * T, :] = dot(p, On[rows, :], NN).astype(bf16)
        dqt[:, rows] = dot(kr.T, ds, NN)
    for c in range(nch):
        ks = slice(c * CHUNK, (c + 1) * CHUNK)
        dk = jnp.zeros((CHUNK, D), f32)
        dv = jnp.zeros((CHUNK, D), f32)
        for r in range(4):
            rows = slice(r * R, (r + 1) * R)
            p = Pm[ks, rows]
            dp = dot(V[ks, :], pack[r, R:2 * R, :], NT)
            ds = (p.astype(f32) * (dp - stat[0:1, rows])).astype(bf16)
            dk = dk + dot(ds, Qn[rows, :], NN)
            dv = dv + dot(p, On[rows, :], NN)
            dqt[:, rows] += dot(KT[:, ks], ds, NN)
        for j in range(CHUNK // spots):
            block = c * (CHUNK // spots) + j
            part = slice(j * spots, (j + 1) * spots)
            out_kvs[block // 4][block % 4, 0] = dk[part, :].astype(bf16)
            out_kvs[block // 4][block % 4, 1] = dv[part, :].astype(bf16)
    for r in range(4):
        rows = slice(r * R, (r + 1) * R)
        out_pack[r, R:2 * R, :] = (dqt[:, rows] * (stat[1:2, rows] * C)).T.astype(bf16)


def attention_call(pack, kvs, rows_per, own_len, head_dim, group):
    spots = kvs[0].shape[2]
    nk = spots * 32
    shapes = [jax.ShapeDtypeStruct(x.shape, bf16) for x in [pack] + list(kvs)]
    rows = 4 * rows_per

    def body(*refs):
        attention_kernel(
            *refs, rows_per=rows_per, own_len=own_len, head_dim=head_dim, group=group, spots=spots
        )

    outs = pl.pallas_call(
        body,
        out_shape=shapes,
        scratch_shapes=[
            pltpu.VMEM((nk, head_dim), bf16),
            pltpu.VMEM((nk, head_dim), bf16),
            pltpu.VMEM((nk + own_len, rows_per), f32),
            pltpu.VMEM((nk + own_len, rows), bf16),
            pltpu.VMEM((head_dim, nk), bf16),
            pltpu.VMEM((head_dim + 16, nk), bf16),
            pltpu.VMEM((rows, head_dim), bf16),
            pltpu.VMEM((rows, head_dim), bf16),
            pltpu.VMEM((8, rows), f32),
            pltpu.VMEM((head_dim, rows), f32),
        ],
        compiler_params=pltpu.CompilerParams(vmem_limit_bytes=40 * 2**20),
        name="attention",
    )(pack, *kvs)
    return outs[0], outs[1:]


def on_device(
    queries, response_keys, response_values, prompt_keys, prompt_value_rows, lengths, grad_out
):
    _, T, H, D = queries.shape
    KH = prompt_keys.shape[1]
    G = H // KH
    R = T * G

    def over_z(x, k):
        return lax.ppermute(x, "z", [(i, (i + k) % 8) for i in range(8)])

    def swap_y(x):
        return lax.all_to_all(x, "y", 0, 0, tiled=True)

    kv = jnp.stack([prompt_keys, prompt_value_rows], axis=0)
    kv = swap_y(jnp.transpose(kv, (2, 0, 1, 3)))

    live = (jnp.arange(T) < lengths[0])[:, None, None]
    masked = jnp.where(live, grad_out[0], jnp.zeros((), bf16))

    def by_head(x, n):
        x = x.reshape(T, KH, n, D)
        return jnp.transpose(x, (1, 0, 2, 3)).reshape(KH, T * n, D)

    pack = jnp.concatenate(
        [
            by_head(queries, G),
            by_head(masked, G),
            by_head(response_keys, 1),
            by_head(response_values, 1),
        ],
        axis=1,
    )
    kv, pack = lax.optimization_barrier((kv, pack))
    pack = swap_y(pack)
    from_2 = over_z(kv, 2)
    from_m2 = over_z(kv, -2)
    from_1 = over_z(kv, 1)
    from_m1 = over_z(kv, -1)
    from_4 = over_z(from_2, 2)
    from_3 = over_z(from_2, 1)
    from_m3 = over_z(from_m2, -1)

    kvs = [kv, from_1, from_m1, from_2, from_m2, from_3, from_m3, from_4]
    pack, dkv = attention_call(pack, kvs, R, T, D, G)

    d0, d1, dm1, d2, dm2, d3, dm3, d4 = dkv
    home = swap_y(pack)
    via_2 = over_z(d4, -2)
    via_1 = over_z(d3, -1)
    via_m1 = over_z(dm3, 1)
    far = (d2.astype(f32) + via_1.astype(f32) + via_2.astype(f32)).astype(bf16)
    far_m = (dm2.astype(f32) + via_m1.astype(f32)).astype(bf16)
    parts = [over_z(d1, -1), over_z(dm1, 1), over_z(far, -2), over_z(far_m, 2)]
    total = d0.astype(f32)
    for x in parts:
        total = total + x.astype(f32)
    total = swap_y(total.astype(bf16))

    def by_token(x, n):
        x = x.reshape(KH, T, n, D)
        return jnp.transpose(x, (1, 0, 2, 3)).reshape(1, T, KH * n, D)

    attended = by_token(home[:, 0:R], G)
    attended = jnp.where(live, attended, jnp.zeros((), bf16))
    return (
        attended,
        by_token(home[:, R:2 * R], G),
        by_token(home[:, 2 * R:2 * R + T], 1),
        by_token(home[:, 2 * R + T:2 * R + 2 * T], 1),
        jnp.transpose(total[:, 0], (1, 0, 2)),
        jnp.transpose(total[:, 1], (1, 0, 2)),
    )


def solution(mesh):
    split = Mesh(mesh.devices.reshape(8, 8, 4), ("batch", "z", "y"))
    spec = P(("batch", "z", "y"))
    return jax.shard_map(
        on_device,
        mesh=split,
        in_specs=(spec,) * 7,
        out_specs=(spec,) * 6,
        check_vma=False,
    )
```

```python
import jax
import jax.numpy as jnp
from jax import lax
from jax.experimental import pallas as pl
from jax.experimental.pallas import tpu as pltpu
from jax.sharding import Mesh, PartitionSpec as P

LOG2E = 1.4426950408889634
CHUNK = 512
f32 = jnp.float32
bf16 = jnp.bfloat16
NT = (((1,), (1,)), ((), ()))
NN = (((1,), (0,)), ((), ()))


def dot(a, b, dims):
    return lax.dot_general(a, b, dims, preferred_element_type=f32)


def attention_kernel(*refs, rows_per, own_len, head_dim, group, spots):
    pack = refs[0]
    kvs = refs[1:9]
    out_pack = refs[9]
    out_kvs = refs[10:18]
    K, V, S, Pm, KT, VT, Qn, On, stat, dqt = refs[18:]
    R = rows_per
    T = own_len
    D = head_dim
    C = D ** (-0.5)
    nk = K.shape[0]
    nch = nk // CHUNK
    for i in range(8):
        for j in range(4):
            at = (4 * i + j) * spots
            K[at:at + spots, :] = kvs[i][j, 0]
            V[at:at + spots, :] = kvs[i][j, 1]
    for c in range(nch):
        KT[:, c * CHUNK:(c + 1) * CHUNK] = K[c * CHUNK:(c + 1) * CHUNK, :].T
        VT[0:D, c * CHUNK:(c + 1) * CHUNK] = V[c * CHUNK:(c + 1) * CHUNK, :].T
    VT[D:D + 16, :] = jnp.ones((16, nk), bf16)
    key_pos = lax.broadcasted_iota(jnp.int32, (T, R), 0)
    row_pos = lax.broadcasted_iota(jnp.int32, (T, R), 1) // group
    for r in range(4):
        rows = slice(r * R, (r + 1) * R)
        qr = pack[r, 0:R, :]
        dor = pack[r, R:2 * R, :]
        kr = pack[r, 2 * R:2 * R + T, :]
        vr = pack[r, 2 * R + T:2 * R + 2 * T, :]
        top = jnp.full((8, R), -jnp.inf, f32)
        for c in range(nch):
            s = dot(K[c * CHUNK:(c + 1) * CHUNK, :], qr, NT)
            S[c * CHUNK:(c + 1) * CHUNK, :] = s
            top = jnp.maximum(top, jnp.max(s.reshape(CHUNK // 8, 8, R), axis=0))
        s = dot(kr, qr, NT)
        s = jnp.where(key_pos <= row_pos, s, -1e30)
        S[nk:nk + T, :] = s
        top = jnp.maximum(top, jnp.max(s.reshape(T // 8, 8, R), axis=0))
        top = jnp.max(top, axis=0, keepdims=True) * (C * LOG2E)
        acc = jnp.zeros((D + 16, R), f32)
        for c in range(nch):
            p = jnp.exp2(S[c * CHUNK:(c + 1) * CHUNK, :] * (C * LOG2E) - top).astype(bf16)
            Pm[c * CHUNK:(c + 1) * CHUNK, rows] = p
            acc = acc + dot(VT[:, c * CHUNK:(c + 1) * CHUNK], p, NN)
        p = jnp.exp2(S[nk:nk + T, :] * (C * LOG2E) - top).astype(bf16)
        Pm[nk:nk + T, rows] = p
        acc = acc + dot(jnp.concatenate([vr.T, jnp.ones((16, T), bf16)], axis=0), p, NN)
        inv = 1.0 / acc[D:D + 1, :]
        o = (acc[0:D, :] * inv).T.astype(bf16)
        out_pack[r, 0:R, :] = o
        dof = dor.astype(f32)
        delta = jnp.sum(dof * o.astype(f32), axis=1, keepdims=True)
        stat[0:1, rows] = jnp.broadcast_to(delta, (R, D)).T[0:1, :]
        stat[1:2, rows] = inv
        inv_col = jnp.broadcast_to(inv, (D, R)).T
        Qn[rows, :] = (qr.astype(f32) * (inv_col * C)).astype(bf16)
        On[rows, :] = (dof * inv_col).astype(bf16)
    for r in range(4):
        rows = slice(r * R, (r + 1) * R)
        dor = pack[r, R:2 * R, :]
        kr = pack[r, 2 * R:2 * R + T, :]
        vr = pack[r, 2 * R + T:2 * R + 2 * T, :]
        p = Pm[nk:nk + T, rows]
        ds = (p.astype(f32) * (dot(vr, dor, NT) - stat[0:1, rows])).astype(bf16)
        out_pack[r, 2 * R:2 * R + T, :] = dot(ds, Qn[rows, :], NN).astype(bf16)
        out_pack[r, 2 * R + T:2 * R + 2 * T, :] = dot(p, On[rows, :], NN).astype(bf16)
        dqt[:, rows] = dot(kr.T, ds, NN)
    for c in range(nch):
        ks = slice(c * CHUNK, (c + 1) * CHUNK)
        dk = jnp.zeros((CHUNK, D), f32)
        dv = jnp.zeros((CHUNK, D), f32)
        for r in range(4):
            rows = slice(r * R, (r + 1) * R)
            p = Pm[ks, rows]
            dp = dot(V[ks, :], pack[r, R:2 * R, :], NT)
            ds = (p.astype(f32) * (dp - stat[0:1, rows])).astype(bf16)
            dk = dk + dot(ds, Qn[rows, :], NN)
            dv = dv + dot(p, On[rows, :], NN)
            dqt[:, rows] += dot(KT[:, ks], ds, NN)
        for j in range(CHUNK // spots):
            block = c * (CHUNK // spots) + j
            part = slice(j * spots, (j + 1) * spots)
            out_kvs[block // 4][block % 4, 0] = dk[part, :].astype(bf16)
            out_kvs[block // 4][block % 4, 1] = dv[part, :].astype(bf16)
    for r in range(4):
        rows = slice(r * R, (r + 1) * R)
        out_pack[r, R:2 * R, :] = (dqt[:, rows] * (stat[1:2, rows] * C)).T.astype(bf16)


def attention_call(pack, kvs, rows_per, own_len, head_dim, group):
    spots = kvs[0].shape[2]
    nk = spots * 32
    shapes = [jax.ShapeDtypeStruct(x.shape, bf16) for x in [pack] + list(kvs)]
    rows = 4 * rows_per

    def body(*refs):
        attention_kernel(
            *refs, rows_per=rows_per, own_len=own_len, head_dim=head_dim, group=group, spots=spots
        )

    outs = pl.pallas_call(
        body,
        out_shape=shapes,
        scratch_shapes=[
            pltpu.VMEM((nk, head_dim), bf16),
            pltpu.VMEM((nk, head_dim), bf16),
            pltpu.VMEM((nk + own_len, rows_per), f32),
            pltpu.VMEM((nk + own_len, rows), bf16),
            pltpu.VMEM((head_dim, nk), bf16),
            pltpu.VMEM((head_dim + 16, nk), bf16),
            pltpu.VMEM((rows, head_dim), bf16),
            pltpu.VMEM((rows, head_dim), bf16),
            pltpu.VMEM((8, rows), f32),
            pltpu.VMEM((head_dim, rows), f32),
        ],
        compiler_params=pltpu.CompilerParams(vmem_limit_bytes=40 * 2**20),
        name="attention",
    )(pack, *kvs)
    return outs[0], outs[1:]


def on_device(
    queries, response_keys, response_values, prompt_keys, prompt_value_rows, lengths, grad_out
):
    _, T, H, D = queries.shape
    KH = prompt_keys.shape[1]
    G = H // KH
    R = T * G

    def over_z(x, k):
        return lax.ppermute(x, "z", [(i, (i + k) % 8) for i in range(8)])

    def swap_y(x):
        return lax.all_to_all(x, "y", 0, 0, tiled=True)

    kv = jnp.stack([prompt_keys, prompt_value_rows], axis=0)
    kv = swap_y(jnp.transpose(kv, (2, 0, 1, 3)))

    live = (jnp.arange(T) < lengths[0])[:, None, None]
    masked = jnp.where(live, grad_out[0], jnp.zeros((), bf16))

    def by_head(x, n):
        x = x.reshape(T, KH, n, D)
        return jnp.transpose(x, (1, 0, 2, 3)).reshape(KH, T * n, D)

    pack = jnp.concatenate(
        [
            by_head(queries, G),
            by_head(masked, G),
            by_head(response_keys, 1),
            by_head(response_values, 1),
        ],
        axis=1,
    )
    kv, pack = lax.optimization_barrier((kv, pack))
    pack = swap_y(pack)
    from_2 = over_z(kv, 2)
    from_m2 = over_z(kv, -2)
    from_1 = over_z(kv, 1)
    from_m1 = over_z(kv, -1)
    from_4 = over_z(from_2, 2)
    from_3 = over_z(from_2, 1)
    from_m3 = over_z(from_m2, -1)

    kvs = [kv, from_1, from_m1, from_2, from_m2, from_3, from_m3, from_4]
    pack, dkv = attention_call(pack, kvs, R, T, D, G)

    d0, d1, dm1, d2, dm2, d3, dm3, d4 = dkv
    home = swap_y(pack)
    via_2 = over_z(d4, -2)
    via_1 = over_z(d3, -1)
    via_m1 = over_z(dm3, 1)
    far = (d2.astype(f32) + via_1.astype(f32) + via_2.astype(f32)).astype(bf16)
    far_m = (dm2.astype(f32) + via_m1.astype(f32)).astype(bf16)
    parts = [over_z(d1, -1), over_z(dm1, 1), over_z(far, -2), over_z(far_m, 2)]
    total = d0.astype(f32)
    for x in parts:
        total = total + x.astype(f32)
    total, home = lax.optimization_barrier((total.astype(bf16), home))
    total = swap_y(total)

    def by_token(x, n):
        x = x.reshape(KH, T, n, D)
        return jnp.transpose(x, (1, 0, 2, 3)).reshape(1, T, KH * n, D)

    attended = by_token(home[:, 0:R], G)
    attended = jnp.where(live, attended, jnp.zeros((), bf16))
    return (
        attended,
        by_token(home[:, R:2 * R], G),
        by_token(home[:, 2 * R:2 * R + T], 1),
        by_token(home[:, 2 * R + T:2 * R + 2 * T], 1),
        jnp.transpose(total[:, 0], (1, 0, 2)),
        jnp.transpose(total[:, 1], (1, 0, 2)),
    )


def solution(mesh):
    split = Mesh(mesh.devices.reshape(8, 8, 4), ("batch", "z", "y"))
    spec = P(("batch", "z", "y"))
    return jax.shard_map(
        on_device,
        mesh=split,
        in_specs=(spec,) * 7,
        out_specs=(spec,) * 6,
        check_vma=False,
    )
```

```python
import functools

import jax
import jax.numpy as jnp
from jax import lax
from jax.experimental import pallas as pl
from jax.experimental.pallas import tpu as pltpu
from jax.sharding import Mesh, PartitionSpec as P

LOG2E = 1.4426950408889634
CHUNK = 512
f32 = jnp.float32
bf16 = jnp.bfloat16
NT = (((1,), (1,)), ((), ()))
NN = (((1,), (0,)), ((), ()))


def dot(a, b, dims):
    return lax.dot_general(a, b, dims, preferred_element_type=f32)


def spans(total, size):
    return [slice(i, min(i + size, total)) for i in range(0, total, size)]


def load_blocks(kvs, K, V, KT, VT):
    spots, D = kvs[0].shape[2], kvs[0].shape[3]
    for i in range(len(kvs)):
        for j in range(4):
            at = (4 * i + j) * spots
            K[at:at + spots, :] = kvs[i][j, 0]
            V[at:at + spots, :] = kvs[i][j, 1]
    for ks in spans(K.shape[0], CHUNK):
        if KT is not None:
            KT[:, ks] = K[ks, :].T
        if VT is not None:
            VT[0:D, ks] = V[ks, :].T
    if VT is not None:
        VT[D:D + 16, :] = jnp.ones((16, K.shape[0]), bf16)


def store_blocks(out_kvs, ks, dk, dv):
    spots = out_kvs[0].shape[2]
    for j in range((ks.stop - ks.start) // spots):
        block = ks.start // spots + j
        part = slice(j * spots, (j + 1) * spots)
        out_kvs[block // 4][block % 4, 0] = dk[part, :].astype(bf16)
        out_kvs[block // 4][block % 4, 1] = dv[part, :].astype(bf16)


def scores_into(S, at, s, top):
    S[at, :] = s
    return jnp.maximum(top, jnp.max(s.reshape(s.shape[0] // 8, 8, s.shape[1]), axis=0))


def near_forward(pack, kv0, kv1, kv2, kv3, kv4, Pm, acc_ref, top_ref, K, V, S, VT, *, T, G):
    D = K.shape[1]
    R = T * G
    C = D ** (-0.5)
    nk = K.shape[0]
    load_blocks((kv0, kv1, kv2, kv3, kv4), K, V, None, VT)
    key_pos = lax.broadcasted_iota(jnp.int32, (T, R), 0)
    row_pos = lax.broadcasted_iota(jnp.int32, (T, R), 1) // G
    own = slice(nk, nk + T)
    for r in range(4):
        rows = slice(r * R, (r + 1) * R)
        qr = pack[r, 0:R, :]
        kr = pack[r, 2 * R:2 * R + T, :]
        vr = pack[r, 2 * R + T:2 * R + 2 * T, :]
        top = jnp.full((8, R), -jnp.inf, f32)
        for ks in spans(nk, CHUNK):
            top = scores_into(S, ks, dot(K[ks, :], qr, NT), top)
        s = jnp.where(key_pos <= row_pos, dot(kr, qr, NT), -1e30)
        top = scores_into(S, own, s, top)
        top = jnp.max(top, axis=0, keepdims=True) * (C * LOG2E)
        top_ref[0:1, rows] = top
        p = jnp.exp2(S[own, :] * (C * LOG2E) - top).astype(bf16)
        Pm[own, rows] = p
        acc = dot(jnp.concatenate([vr.T, jnp.ones((16, T), bf16)], axis=0), p, NN)
        for ks in spans(nk, CHUNK):
            p = jnp.exp2(S[ks, :] * (C * LOG2E) - top).astype(bf16)
            Pm[ks, rows] = p
            acc = acc + dot(VT[:, ks], p, NN)
        acc_ref[:, rows] = acc


def far_both(
    pack, kv0, kv1, kv2, acc_ref, top_ref, o_ref, stat, Qs, Os, dqt, d0, d1, d2,
    K, V, S, Pm, KT, VT, Qn, On, *, T, G
):
    D = K.shape[1]
    R = T * G
    C = D ** (-0.5)
    nk = K.shape[0]
    load_blocks((kv0, kv1, kv2), K, V, KT, VT)
    for r in range(4):
        rows = slice(r * R, (r + 1) * R)
        qr = pack[r, 0:R, :]
        dof = pack[r, R:2 * R, :].astype(f32)
        top = jnp.full((8, R), -jnp.inf, f32)
        for ks in spans(nk, CHUNK):
            top = scores_into(S, ks, dot(K[ks, :], qr, NT), top)
        near_top = top_ref[0:1, rows]
        top = jnp.maximum(near_top, jnp.max(top, axis=0, keepdims=True) * (C * LOG2E))
        near = jnp.exp2(near_top - top)
        acc = acc_ref[:, rows] * near
        for ks in spans(nk, CHUNK):
            p = jnp.exp2(S[ks, :] * (C * LOG2E) - top).astype(bf16)
            Pm[ks, rows] = p
            acc = acc + dot(VT[:, ks], p, NN)
        inv = 1.0 / acc[D:D + 1, :]
        o = (acc[0:D, :] * inv).T.astype(bf16)
        o_ref[r] = o
        delta = jnp.sum(dof * o.astype(f32), axis=1, keepdims=True)
        stat[0:1, rows] = jnp.broadcast_to(delta, (R, D)).T[0:1, :]
        stat[1:2, rows] = inv
        stat[2:3, rows] = inv * near
        inv_col = jnp.broadcast_to(inv, (D, R)).T
        near_col = jnp.broadcast_to(inv * near, (D, R)).T
        qf = qr.astype(f32) * C
        Qn[rows, :] = (qf * inv_col).astype(bf16)
        On[rows, :] = (dof * inv_col).astype(bf16)
        Qs[rows, :] = (qf * near_col).astype(bf16)
        Os[rows, :] = (dof * near_col).astype(bf16)
    for i, ks in enumerate(spans(nk, CHUNK)):
        dk = jnp.zeros((ks.stop - ks.start, D), f32)
        dv = jnp.zeros((ks.stop - ks.start, D), f32)
        for r in range(4):
            rows = slice(r * R, (r + 1) * R)
            p = Pm[ks, rows]
            dp = dot(V[ks, :], pack[r, R:2 * R, :], NT)
            ds = (p.astype(f32) * (dp - stat[0:1, rows])).astype(bf16)
            dk = dk + dot(ds, Qn[rows, :], NN)
            dv = dv + dot(p, On[rows, :], NN)
            part = dot(KT[:, ks], ds, NN) * stat[1:2, rows]
            if i == 0:
                dqt[:, rows] = part
            else:
                dqt[:, rows] += part
        store_blocks((d0, d1, d2), ks, dk, dv)


def near_backward(
    pack, kv0, kv1, kv2, kv3, kv4, Pm, o_ref, stat, Qs, Os, dqt, out, d0, d1, d2, d3, d4,
    K, V, KT, acc, *, T, G
):
    D = K.shape[1]
    R = T * G
    C = D ** (-0.5)
    nk = K.shape[0]
    load_blocks((kv0, kv1, kv2, kv3, kv4), K, V, KT, None)
    own = slice(nk, nk + T)
    for r in range(4):
        rows = slice(r * R, (r + 1) * R)
        kr = pack[r, 2 * R:2 * R + T, :]
        vr = pack[r, 2 * R + T:2 * R + 2 * T, :]
        p = Pm[own, rows]
        ds = (p.astype(f32) * (dot(vr, pack[r, R:2 * R, :], NT) - stat[0:1, rows])).astype(bf16)
        out[r, 0:R, :] = o_ref[r]
        out[r, 2 * R:2 * R + T, :] = dot(ds, Qs[rows, :], NN).astype(bf16)
        out[r, 2 * R + T:2 * R + 2 * T, :] = dot(p, Os[rows, :], NN).astype(bf16)
        acc[:, rows] = dot(kr.T, ds, NN)
    for ks in spans(nk, CHUNK):
        dk = jnp.zeros((ks.stop - ks.start, D), f32)
        dv = jnp.zeros((ks.stop - ks.start, D), f32)
        for r in range(4):
            rows = slice(r * R, (r + 1) * R)
            p = Pm[ks, rows]
            dp = dot(V[ks, :], pack[r, R:2 * R, :], NT)
            ds = (p.astype(f32) * (dp - stat[0:1, rows])).astype(bf16)
            dk = dk + dot(ds, Qs[rows, :], NN)
            dv = dv + dot(p, Os[rows, :], NN)
            acc[:, rows] += dot(KT[:, ks], ds, NN)
        store_blocks((d0, d1, d2, d3, d4), ks, dk, dv)
    for r in range(4):
        rows = slice(r * R, (r + 1) * R)
        dq = (dqt[:, rows] + acc[:, rows] * stat[2:3, rows]) * C
        out[r, R:2 * R, :] = dq.T.astype(bf16)


def call(body, name, out_shape, scratch, flops, *args):
    return pl.pallas_call(
        body,
        out_shape=out_shape,
        scratch_shapes=scratch,
        compiler_params=pltpu.CompilerParams(vmem_limit_bytes=32 * 2**20),
        cost_estimate=pl.CostEstimate(flops=flops, bytes_accessed=4 * 2**20, transcendentals=0),
        name=name,
    )(*args)


def on_device(
    queries, response_keys, response_values, prompt_keys, prompt_value_rows, lengths, grad_out
):
    _, T, H, D = queries.shape
    KH = prompt_keys.shape[1]
    G = H // KH
    R = T * G

    def over_z(x, k):
        return lax.ppermute(x, "z", [(i, (i + k) % 8) for i in range(8)])

    def swap_y(x):
        return lax.all_to_all(x, "y", 0, 0, tiled=True)

    kv = jnp.stack([prompt_keys, prompt_value_rows], axis=0)
    kv = swap_y(jnp.transpose(kv, (2, 0, 1, 3)))

    live = (jnp.arange(T) < lengths[0])[:, None, None]
    masked = jnp.where(live, grad_out[0], jnp.zeros((), bf16))

    def by_head(x, n):
        x = x.reshape(T, KH, n, D)
        return jnp.transpose(x, (1, 0, 2, 3)).reshape(KH, T * n, D)

    pack = jnp.concatenate(
        [
            by_head(queries, G),
            by_head(masked, G),
            by_head(response_keys, 1),
            by_head(response_values, 1),
        ],
        axis=1,
    )
    kv, pack = lax.optimization_barrier((kv, pack))
    pack = swap_y(pack)
    from_2 = over_z(kv, 2)
    from_m2 = over_z(kv, -2)
    from_1 = over_z(kv, 1)
    from_m1 = over_z(kv, -1)
    from_4 = over_z(from_2, 2)
    from_3 = over_z(from_2, 1)
    from_m3 = over_z(from_m2, -1)

    near = (kv, from_1, from_m1, from_2, from_m2)
    far = (from_3, from_m3, from_4)
    block = jax.ShapeDtypeStruct(kv.shape, bf16)
    spots = kv.shape[2]
    near_keys = 5 * 4 * spots
    far_keys = 3 * 4 * spots
    rows = 4 * R

    def shape(dims, kind):
        return jax.ShapeDtypeStruct(dims, kind)

    def cost(products, keys):
        return products * 2 * rows * keys * D

    weights, acc, top = call(
        functools.partial(near_forward, T=T, G=G),
        "near_forward",
        (
            shape((near_keys + T, rows), bf16),
            shape((D + 16, rows), f32),
            shape((8, rows), f32),
        ),
        [
            pltpu.VMEM((near_keys, D), bf16),
            pltpu.VMEM((near_keys, D), bf16),
            pltpu.VMEM((near_keys + T, R), f32),
            pltpu.VMEM((D + 16, near_keys), bf16),
        ],
        cost(2, near_keys + T),
        pack, *near,
    )
    out, stat, q_near, g_near, dqt, d3, dm3, d4 = call(
        functools.partial(far_both, T=T, G=G),
        "far_both",
        (
            shape((4, R, D), bf16),
            shape((8, rows), f32),
            shape((rows, D), bf16),
            shape((rows, D), bf16),
            shape((D, rows), f32),
            block, block, block,
        ),
        [
            pltpu.VMEM((far_keys, D), bf16),
            pltpu.VMEM((far_keys, D), bf16),
            pltpu.VMEM((far_keys, R), f32),
            pltpu.VMEM((far_keys, rows), bf16),
            pltpu.VMEM((D, far_keys), bf16),
            pltpu.VMEM((D + 16, far_keys), bf16),
            pltpu.VMEM((rows, D), bf16),
            pltpu.VMEM((rows, D), bf16),
        ],
        cost(6, far_keys),
        pack, *far, acc, top,
    )
    home, d0, d1, dm1, d2, dm2 = call(
        functools.partial(near_backward, T=T, G=G),
        "near_backward",
        (shape(pack.shape, bf16), block, block, block, block, block),
        [
            pltpu.VMEM((near_keys, D), bf16),
            pltpu.VMEM((near_keys, D), bf16),
            pltpu.VMEM((D, near_keys), bf16),
            pltpu.VMEM((D, rows), f32),
        ],
        cost(4, near_keys + T),
        pack, *near, weights, out, stat, q_near, g_near, dqt,
    )
    home = swap_y(home)
    via_2 = over_z(d4, -2)
    via_1 = over_z(d3, -1)
    via_m1 = over_z(dm3, 1)
    far = (d2.astype(f32) + via_1.astype(f32) + via_2.astype(f32)).astype(bf16)
    far_m = (dm2.astype(f32) + via_m1.astype(f32)).astype(bf16)
    parts = [over_z(d1, -1), over_z(dm1, 1), over_z(far, -2), over_z(far_m, 2)]
    total = d0.astype(f32)
    for x in parts:
        total = total + x.astype(f32)
    total, home = lax.optimization_barrier((total.astype(bf16), home))
    total = swap_y(total)

    def by_token(x, n):
        x = x.reshape(KH, T, n, D)
        return jnp.transpose(x, (1, 0, 2, 3)).reshape(1, T, KH * n, D)

    attended = by_token(home[:, 0:R], G)
    attended = jnp.where(live, attended, jnp.zeros((), bf16))
    return (
        attended,
        by_token(home[:, R:2 * R], G),
        by_token(home[:, 2 * R:2 * R + T], 1),
        by_token(home[:, 2 * R + T:2 * R + 2 * T], 1),
        jnp.transpose(total[:, 0], (1, 0, 2)),
        jnp.transpose(total[:, 1], (1, 0, 2)),
    )


def solution(mesh):
    split = Mesh(mesh.devices.reshape(8, 8, 4), ("batch", "z", "y"))
    spec = P(("batch", "z", "y"))
    return jax.shard_map(
        on_device,
        mesh=split,
        in_specs=(spec,) * 7,
        out_specs=(spec,) * 6,
        check_vma=False,
    )
```

```python
import functools

import jax
import jax.numpy as jnp
from jax import lax
from jax.experimental import pallas as pl
from jax.experimental.pallas import tpu as pltpu
from jax.sharding import Mesh, PartitionSpec as P

LOG2E = 1.4426950408889634
CHUNK = 512
f32 = jnp.float32
bf16 = jnp.bfloat16
NT = (((1,), (1,)), ((), ()))
NN = (((1,), (0,)), ((), ()))


def dot(a, b, dims):
    return lax.dot_general(a, b, dims, preferred_element_type=f32)


def spans(total, size):
    return [slice(i, min(i + size, total)) for i in range(0, total, size)]


def load_blocks(kvs, K, V, KT, VT):
    spots, D = kvs[0].shape[2], kvs[0].shape[3]
    for i in range(len(kvs)):
        for j in range(4):
            at = (4 * i + j) * spots
            K[at:at + spots, :] = kvs[i][j, 0]
            V[at:at + spots, :] = kvs[i][j, 1]
    for ks in spans(K.shape[0], CHUNK):
        if KT is not None:
            KT[:, ks] = K[ks, :].T
        if VT is not None:
            VT[0:D, ks] = V[ks, :].T
    if VT is not None:
        VT[D:D + 16, :] = jnp.ones((16, K.shape[0]), bf16)


def store_blocks(out_kvs, ks, dk, dv):
    spots = out_kvs[0].shape[2]
    for j in range((ks.stop - ks.start) // spots):
        block = ks.start // spots + j
        part = slice(j * spots, (j + 1) * spots)
        out_kvs[block // 4][block % 4, 0] = dk[part, :].astype(bf16)
        out_kvs[block // 4][block % 4, 1] = dv[part, :].astype(bf16)


def scores_into(S, at, s, top):
    S[at, :] = s
    return jnp.maximum(top, jnp.max(s.reshape(s.shape[0] // 8, 8, s.shape[1]), axis=0))


def near_forward(pack, kv0, kv1, kv2, kv3, kv4, Pm, acc_ref, top_ref, K, V, S, VT, *, T, G):
    D = K.shape[1]
    R = T * G
    C = D ** (-0.5)
    nk = K.shape[0]
    load_blocks((kv0, kv1, kv2, kv3, kv4), K, V, None, VT)
    key_pos = lax.broadcasted_iota(jnp.int32, (T, R), 0)
    row_pos = lax.broadcasted_iota(jnp.int32, (T, R), 1) // G
    own = slice(nk, nk + T)
    for r in range(4):
        rows = slice(r * R, (r + 1) * R)
        qr = pack[r, 0:R, :]
        kr = pack[r, 2 * R:2 * R + T, :]
        vr = pack[r, 2 * R + T:2 * R + 2 * T, :]
        top = jnp.full((8, R), -jnp.inf, f32)
        for ks in spans(nk, CHUNK):
            top = scores_into(S, ks, dot(K[ks, :], qr, NT), top)
        s = jnp.where(key_pos <= row_pos, dot(kr, qr, NT), -1e30)
        top = scores_into(S, own, s, top)
        top = jnp.max(top, axis=0, keepdims=True) * (C * LOG2E)
        top_ref[0:1, rows] = top
        p = jnp.exp2(S[own, :] * (C * LOG2E) - top).astype(bf16)
        Pm[own, rows] = p
        acc = dot(jnp.concatenate([vr.T, jnp.ones((16, T), bf16)], axis=0), p, NN)
        for ks in spans(nk, CHUNK):
            p = jnp.exp2(S[ks, :] * (C * LOG2E) - top).astype(bf16)
            Pm[ks, rows] = p
            acc = acc + dot(VT[:, ks], p, NN)
        acc_ref[:, rows] = acc


def far_both(
    pack, kv0, kv1, kv2, acc_ref, top_ref, o_ref, stat, Qs, Os, dqt, d0, d1, d2,
    K, V, S, Pm, KT, VT, Qn, On, *, T, G
):
    D = K.shape[1]
    R = T * G
    C = D ** (-0.5)
    nk = K.shape[0]
    load_blocks((kv0, kv1, kv2), K, V, KT, VT)
    for r in range(4):
        rows = slice(r * R, (r + 1) * R)
        qr = pack[r, 0:R, :]
        dof = pack[r, R:2 * R, :].astype(f32)
        top = jnp.full((8, R), -jnp.inf, f32)
        for ks in spans(nk, CHUNK):
            top = scores_into(S, ks, dot(K[ks, :], qr, NT), top)
        near_top = top_ref[0:1, rows]
        top = jnp.maximum(near_top, jnp.max(top, axis=0, keepdims=True) * (C * LOG2E))
        near = jnp.exp2(near_top - top)
        acc = acc_ref[:, rows] * near
        for ks in spans(nk, CHUNK):
            p = jnp.exp2(S[ks, :] * (C * LOG2E) - top).astype(bf16)
            Pm[ks, rows] = p
            acc = acc + dot(VT[:, ks], p, NN)
        inv = 1.0 / acc[D:D + 1, :]
        o = (acc[0:D, :] * inv).T.astype(bf16)
        o_ref[r] = o
        delta = jnp.sum(dof * o.astype(f32), axis=1, keepdims=True)
        stat[0:1, rows] = jnp.broadcast_to(delta, (R, D)).T[0:1, :]
        stat[1:2, rows] = inv
        stat[2:3, rows] = inv * near
        inv_col = jnp.broadcast_to(inv, (D, R)).T
        near_col = jnp.broadcast_to(inv * near, (D, R)).T
        qf = qr.astype(f32) * C
        Qn[rows, :] = (qf * inv_col).astype(bf16)
        On[rows, :] = (dof * inv_col).astype(bf16)
        Qs[rows, :] = (qf * near_col).astype(bf16)
        Os[rows, :] = (dof * near_col).astype(bf16)
    for i, ks in enumerate(spans(nk, CHUNK)):
        dk = jnp.zeros((ks.stop - ks.start, D), f32)
        dv = jnp.zeros((ks.stop - ks.start, D), f32)
        for r in range(4):
            rows = slice(r * R, (r + 1) * R)
            p = Pm[ks, rows]
            dp = dot(V[ks, :], pack[r, R:2 * R, :], NT)
            ds = (p.astype(f32) * (dp - stat[0:1, rows])).astype(bf16)
            dk = dk + dot(ds, Qn[rows, :], NN)
            dv = dv + dot(p, On[rows, :], NN)
            part = dot(KT[:, ks], ds, NN) * stat[1:2, rows]
            if i == 0:
                dqt[:, rows] = part
            else:
                dqt[:, rows] += part
        store_blocks((d0, d1, d2), ks, dk, dv)


def near_backward(
    pack, kv0, kv1, kv2, kv3, kv4, Pm, o_ref, stat, Qs, Os, dqt, out, d0, d1, d2, d3, d4,
    K, V, KT, acc, *, T, G
):
    D = K.shape[1]
    R = T * G
    C = D ** (-0.5)
    nk = K.shape[0]
    load_blocks((kv0, kv1, kv2, kv3, kv4), K, V, KT, None)
    own = slice(nk, nk + T)
    for r in range(4):
        rows = slice(r * R, (r + 1) * R)
        kr = pack[r, 2 * R:2 * R + T, :]
        vr = pack[r, 2 * R + T:2 * R + 2 * T, :]
        p = Pm[own, rows]
        ds = (p.astype(f32) * (dot(vr, pack[r, R:2 * R, :], NT) - stat[0:1, rows])).astype(bf16)
        out[r, 0:R, :] = o_ref[r]
        out[r, 2 * R:2 * R + T, :] = dot(ds, Qs[rows, :], NN).astype(bf16)
        out[r, 2 * R + T:2 * R + 2 * T, :] = dot(p, Os[rows, :], NN).astype(bf16)
        acc[:, rows] = dot(kr.T, ds, NN)
    for ks in spans(nk, CHUNK):
        dk = jnp.zeros((ks.stop - ks.start, D), f32)
        dv = jnp.zeros((ks.stop - ks.start, D), f32)
        for r in range(4):
            rows = slice(r * R, (r + 1) * R)
            p = Pm[ks, rows]
            dp = dot(V[ks, :], pack[r, R:2 * R, :], NT)
            ds = (p.astype(f32) * (dp - stat[0:1, rows])).astype(bf16)
            dk = dk + dot(ds, Qs[rows, :], NN)
            dv = dv + dot(p, Os[rows, :], NN)
            acc[:, rows] += dot(KT[:, ks], ds, NN)
        store_blocks((d0, d1, d2, d3, d4), ks, dk, dv)
    for r in range(4):
        rows = slice(r * R, (r + 1) * R)
        dq = (dqt[:, rows] + acc[:, rows] * stat[2:3, rows]) * C
        out[r, R:2 * R, :] = dq.T.astype(bf16)


def call(body, name, out_shape, scratch, flops, *args):
    return pl.pallas_call(
        body,
        out_shape=out_shape,
        scratch_shapes=scratch,
        compiler_params=pltpu.CompilerParams(vmem_limit_bytes=32 * 2**20),
        cost_estimate=pl.CostEstimate(flops=flops, bytes_accessed=4 * 2**20, transcendentals=0),
        name=name,
    )(*args)


def on_device(
    queries, response_keys, response_values, prompt_keys, prompt_value_rows, lengths, grad_out
):
    _, T, H, D = queries.shape
    KH = prompt_keys.shape[1]
    G = H // KH
    R = T * G

    def over_z(x, k):
        return lax.ppermute(x, "z", [(i, (i + k) % 8) for i in range(8)])

    def swap_y(x):
        return lax.all_to_all(x, "y", 0, 0, tiled=True)

    kv = jnp.stack([prompt_keys, prompt_value_rows], axis=0)
    kv = swap_y(jnp.transpose(kv, (2, 0, 1, 3)))

    live = (jnp.arange(T) < lengths[0])[:, None, None]
    masked = jnp.where(live, grad_out[0], jnp.zeros((), bf16))

    def by_head(x, n):
        x = x.reshape(T, KH, n, D)
        return jnp.transpose(x, (1, 0, 2, 3)).reshape(KH, T * n, D)

    pack = jnp.concatenate(
        [
            by_head(queries, G),
            by_head(masked, G),
            by_head(response_keys, 1),
            by_head(response_values, 1),
        ],
        axis=1,
    )
    kv, pack = lax.optimization_barrier((kv, pack))
    pack = swap_y(pack)
    from_2 = over_z(kv, 2)
    from_m2 = over_z(kv, -2)
    from_1 = over_z(kv, 1)
    from_m1 = over_z(kv, -1)
    from_4 = over_z(from_2, 2)
    from_3 = over_z(from_2, 1)
    from_m3 = over_z(from_m2, -1)

    near = (kv, from_1, from_m1, from_2, from_m2)
    far = (from_3, from_m3, from_4)
    block = jax.ShapeDtypeStruct(kv.shape, bf16)
    spots = kv.shape[2]
    near_keys = 5 * 4 * spots
    far_keys = 3 * 4 * spots
    rows = 4 * R

    def shape(dims, kind):
        return jax.ShapeDtypeStruct(dims, kind)

    def cost(products, keys):
        return products * 2 * rows * keys * D

    weights, acc, top = call(
        functools.partial(near_forward, T=T, G=G),
        "near_forward",
        (
            shape((near_keys + T, rows), bf16),
            shape((D + 16, rows), f32),
            shape((8, rows), f32),
        ),
        [
            pltpu.VMEM((near_keys, D), bf16),
            pltpu.VMEM((near_keys, D), bf16),
            pltpu.VMEM((near_keys + T, R), f32),
            pltpu.VMEM((D + 16, near_keys), bf16),
        ],
        cost(2, near_keys + T),
        pack, *near,
    )
    out, stat, q_near, g_near, dqt, d3, dm3, d4 = call(
        functools.partial(far_both, T=T, G=G),
        "far_both",
        (
            shape((4, R, D), bf16),
            shape((8, rows), f32),
            shape((rows, D), bf16),
            shape((rows, D), bf16),
            shape((D, rows), f32),
            block, block, block,
        ),
        [
            pltpu.VMEM((far_keys, D), bf16),
            pltpu.VMEM((far_keys, D), bf16),
            pltpu.VMEM((far_keys, R), f32),
            pltpu.VMEM((far_keys, rows), bf16),
            pltpu.VMEM((D, far_keys), bf16),
            pltpu.VMEM((D + 16, far_keys), bf16),
            pltpu.VMEM((rows, D), bf16),
            pltpu.VMEM((rows, D), bf16),
        ],
        cost(6, far_keys),
        pack, *far, acc, top,
    )
    home, d0, d1, dm1, d2, dm2 = call(
        functools.partial(near_backward, T=T, G=G),
        "near_backward",
        (shape(pack.shape, bf16), block, block, block, block, block),
        [
            pltpu.VMEM((near_keys, D), bf16),
            pltpu.VMEM((near_keys, D), bf16),
            pltpu.VMEM((D, near_keys), bf16),
            pltpu.VMEM((D, rows), f32),
        ],
        cost(4, near_keys + T),
        pack, *near, weights, out, stat, q_near, g_near, dqt,
    )
    via_2 = over_z(d4, -2)
    via_1 = over_z(d3, -1)
    via_m1 = over_z(dm3, 1)
    (via_2, via_1, via_m1, home, d1, dm1, d2, dm2) = lax.optimization_barrier(
        (via_2, via_1, via_m1, home, d1, dm1, d2, dm2)
    )
    home = swap_y(home)
    far = (d2.astype(f32) + via_1.astype(f32) + via_2.astype(f32)).astype(bf16)
    far_m = (dm2.astype(f32) + via_m1.astype(f32)).astype(bf16)
    parts = [over_z(d1, -1), over_z(dm1, 1), over_z(far, -2), over_z(far_m, 2)]
    total = d0.astype(f32)
    for x in parts:
        total = total + x.astype(f32)
    total, home = lax.optimization_barrier((total.astype(bf16), home))
    total = swap_y(total)

    def by_token(x, n):
        x = x.reshape(KH, T, n, D)
        return jnp.transpose(x, (1, 0, 2, 3)).reshape(1, T, KH * n, D)

    attended = by_token(home[:, 0:R], G)
    attended = jnp.where(live, attended, jnp.zeros((), bf16))
    return (
        attended,
        by_token(home[:, R:2 * R], G),
        by_token(home[:, 2 * R:2 * R + T], 1),
        by_token(home[:, 2 * R + T:2 * R + 2 * T], 1),
        jnp.transpose(total[:, 0], (1, 0, 2)),
        jnp.transpose(total[:, 1], (1, 0, 2)),
    )


def solution(mesh):
    split = Mesh(mesh.devices.reshape(8, 8, 4), ("batch", "z", "y"))
    spec = P(("batch", "z", "y"))
    return jax.shard_map(
        on_device,
        mesh=split,
        in_specs=(spec,) * 7,
        out_specs=(spec,) * 6,
        check_vma=False,
    )
```

```python
import functools

import jax
import jax.numpy as jnp
from jax import lax
from jax.experimental import pallas as pl
from jax.experimental.pallas import tpu as pltpu
from jax.sharding import Mesh, PartitionSpec as P

LOG2E = 1.4426950408889634
CHUNK = 512
f32 = jnp.float32
bf16 = jnp.bfloat16
NT = (((1,), (1,)), ((), ()))
NN = (((1,), (0,)), ((), ()))


def dot(a, b, dims):
    return lax.dot_general(a, b, dims, preferred_element_type=f32)


def spans(total, size):
    return [slice(i, min(i + size, total)) for i in range(0, total, size)]


def load_blocks(kvs, K, V, KT, VT):
    spots, D = kvs[0].shape[2], kvs[0].shape[3]
    for i in range(len(kvs)):
        for j in range(4):
            at = (4 * i + j) * spots
            K[at:at + spots, :] = kvs[i][j, 0]
            V[at:at + spots, :] = kvs[i][j, 1]
    for ks in spans(K.shape[0], CHUNK):
        if KT is not None:
            KT[:, ks] = K[ks, :].T
        if VT is not None:
            VT[0:D, ks] = V[ks, :].T
    if VT is not None:
        VT[D:D + 16, :] = jnp.ones((16, K.shape[0]), bf16)


def store_blocks(out_kvs, ks, dk, dv):
    spots = out_kvs[0].shape[2]
    for j in range((ks.stop - ks.start) // spots):
        block = ks.start // spots + j
        part = slice(j * spots, (j + 1) * spots)
        out_kvs[block // 4][block % 4, 0] = dk[part, :].astype(bf16)
        out_kvs[block // 4][block % 4, 1] = dv[part, :].astype(bf16)


def scores_into(S, at, s, top):
    S[at, :] = s
    return jnp.maximum(top, jnp.max(s.reshape(s.shape[0] // 8, 8, s.shape[1]), axis=0))


def near_forward(pack, kv0, kv1, kv2, kv3, kv4, Pm, acc_ref, top_ref, K, V, S, VT, *, T, G):
    D = K.shape[1]
    R = T * G
    C = D ** (-0.5)
    nk = K.shape[0]
    load_blocks((kv0, kv1, kv2, kv3, kv4), K, V, None, VT)
    key_pos = lax.broadcasted_iota(jnp.int32, (T, R), 0)
    row_pos = lax.broadcasted_iota(jnp.int32, (T, R), 1) // G
    own = slice(nk, nk + T)
    for r in range(4):
        rows = slice(r * R, (r + 1) * R)
        qr = pack[r, 0:R, :]
        kr = pack[r, 2 * R:2 * R + T, :]
        vr = pack[r, 2 * R + T:2 * R + 2 * T, :]
        top = jnp.full((8, R), -jnp.inf, f32)
        for ks in spans(nk, CHUNK):
            top = scores_into(S, ks, dot(K[ks, :], qr, NT), top)
        s = jnp.where(key_pos <= row_pos, dot(kr, qr, NT), -1e30)
        top = scores_into(S, own, s, top)
        top = jnp.max(top, axis=0, keepdims=True) * (C * LOG2E)
        top_ref[0:1, rows] = top
        p = jnp.exp2(S[own, :] * (C * LOG2E) - top).astype(bf16)
        Pm[own, rows] = p
        acc = dot(jnp.concatenate([vr.T, jnp.ones((16, T), bf16)], axis=0), p, NN)
        for ks in spans(nk, CHUNK):
            p = jnp.exp2(S[ks, :] * (C * LOG2E) - top).astype(bf16)
            Pm[ks, rows] = p
            acc = acc + dot(VT[:, ks], p, NN)
        acc_ref[:, rows] = acc


def far_both(
    pack, kv0, kv1, kv2, acc_ref, top_ref, o_ref, stat, Qs, Os, dqt, d0, d1, d2,
    K, V, S, Pm, KT, VT, Qn, On, *, T, G
):
    D = K.shape[1]
    R = T * G
    C = D ** (-0.5)
    nk = K.shape[0]
    load_blocks((kv0, kv1, kv2), K, V, KT, VT)
    for r in range(4):
        rows = slice(r * R, (r + 1) * R)
        qr = pack[r, 0:R, :]
        dof = pack[r, R:2 * R, :].astype(f32)
        top = jnp.full((8, R), -jnp.inf, f32)
        for ks in spans(nk, CHUNK):
            top = scores_into(S, ks, dot(K[ks, :], qr, NT), top)
        near_top = top_ref[0:1, rows]
        top = jnp.maximum(near_top, jnp.max(top, axis=0, keepdims=True) * (C * LOG2E))
        near = jnp.exp2(near_top - top)
        acc = acc_ref[:, rows] * near
        for ks in spans(nk, CHUNK):
            p = jnp.exp2(S[ks, :] * (C * LOG2E) - top).astype(bf16)
            Pm[ks, rows] = p
            acc = acc + dot(VT[:, ks], p, NN)
        inv = 1.0 / acc[D:D + 1, :]
        o = (acc[0:D, :] * inv).T.astype(bf16)
        o_ref[r] = o
        delta = jnp.sum(dof * o.astype(f32), axis=1, keepdims=True)
        stat[0:1, rows] = jnp.broadcast_to(delta, (R, D)).T[0:1, :]
        stat[1:2, rows] = inv
        stat[2:3, rows] = inv * near
        inv_col = jnp.broadcast_to(inv, (D, R)).T
        near_col = jnp.broadcast_to(inv * near, (D, R)).T
        qf = qr.astype(f32) * C
        Qn[rows, :] = (qf * inv_col).astype(bf16)
        On[rows, :] = (dof * inv_col).astype(bf16)
        Qs[rows, :] = (qf * near_col).astype(bf16)
        Os[rows, :] = (dof * near_col).astype(bf16)
    for i, ks in enumerate(spans(nk, CHUNK)):
        dk = jnp.zeros((ks.stop - ks.start, D), f32)
        dv = jnp.zeros((ks.stop - ks.start, D), f32)
        for r in range(4):
            rows = slice(r * R, (r + 1) * R)
            p = Pm[ks, rows]
            dp = dot(V[ks, :], pack[r, R:2 * R, :], NT)
            ds = (p.astype(f32) * (dp - stat[0:1, rows])).astype(bf16)
            dk = dk + dot(ds, Qn[rows, :], NN)
            dv = dv + dot(p, On[rows, :], NN)
            part = dot(KT[:, ks], ds, NN) * stat[1:2, rows]
            if i == 0:
                dqt[:, rows] = part
            else:
                dqt[:, rows] += part
        store_blocks((d0, d1, d2), ks, dk, dv)


def near_backward(
    pack, kv0, kv1, kv2, kv3, kv4, Pm, o_ref, stat, Qs, Os, dqt, out, d0, d1, d2, d3, d4,
    K, V, KT, acc, *, T, G
):
    D = K.shape[1]
    R = T * G
    C = D ** (-0.5)
    nk = K.shape[0]
    load_blocks((kv0, kv1, kv2, kv3, kv4), K, V, KT, None)
    own = slice(nk, nk + T)
    for r in range(4):
        rows = slice(r * R, (r + 1) * R)
        kr = pack[r, 2 * R:2 * R + T, :]
        vr = pack[r, 2 * R + T:2 * R + 2 * T, :]
        p = Pm[own, rows]
        ds = (p.astype(f32) * (dot(vr, pack[r, R:2 * R, :], NT) - stat[0:1, rows])).astype(bf16)
        out[r, 0:R, :] = o_ref[r]
        out[r, 2 * R:2 * R + T, :] = dot(ds, Qs[rows, :], NN).astype(bf16)
        out[r, 2 * R + T:2 * R + 2 * T, :] = dot(p, Os[rows, :], NN).astype(bf16)
        acc[:, rows] = dot(kr.T, ds, NN)
    for ks in spans(nk, CHUNK):
        dk = jnp.zeros((ks.stop - ks.start, D), f32)
        dv = jnp.zeros((ks.stop - ks.start, D), f32)
        for r in range(4):
            rows = slice(r * R, (r + 1) * R)
            p = Pm[ks, rows]
            dp = dot(V[ks, :], pack[r, R:2 * R, :], NT)
            ds = (p.astype(f32) * (dp - stat[0:1, rows])).astype(bf16)
            dk = dk + dot(ds, Qs[rows, :], NN)
            dv = dv + dot(p, Os[rows, :], NN)
            acc[:, rows] += dot(KT[:, ks], ds, NN)
        store_blocks((d0, d1, d2, d3, d4), ks, dk, dv)
    for r in range(4):
        rows = slice(r * R, (r + 1) * R)
        dq = (dqt[:, rows] + acc[:, rows] * stat[2:3, rows]) * C
        out[r, R:2 * R, :] = dq.T.astype(bf16)


def call(body, name, out_shape, scratch, flops, *args):
    return pl.pallas_call(
        body,
        out_shape=out_shape,
        scratch_shapes=scratch,
        compiler_params=pltpu.CompilerParams(vmem_limit_bytes=32 * 2**20),
        cost_estimate=pl.CostEstimate(flops=flops, bytes_accessed=4 * 2**20, transcendentals=0),
        name=name,
    )(*args)


def on_device(
    queries, response_keys, response_values, prompt_keys, prompt_value_rows, lengths, grad_out
):
    _, T, H, D = queries.shape
    KH = prompt_keys.shape[1]
    G = H // KH
    R = T * G

    def over_z(x, k):
        return lax.ppermute(x, "z", [(i, (i + k) % 8) for i in range(8)])

    def swap_y(x):
        return lax.all_to_all(x, "y", 0, 0, tiled=True)

    def over_y(x, k):
        return lax.ppermute(x, "y", [(i, (i + k) % 4) for i in range(4)])

    def turned(x, by):
        return lax.dynamic_slice_in_dim(jnp.concatenate([x, x], axis=0), by, 4, 0)

    my_y = lax.axis_index("y")
    kv = jnp.stack([prompt_keys, prompt_value_rows], axis=0)
    kv = turned(jnp.transpose(kv, (2, 0, 1, 3)), my_y)
    kv = jnp.stack([kv[0]] + [over_y(kv[k], k) for k in (1, 2, 3)])

    live = (jnp.arange(T) < lengths[0])[:, None, None]
    masked = jnp.where(live, grad_out[0], jnp.zeros((), bf16))

    def by_head(x, n):
        x = x.reshape(T, KH, n, D)
        return jnp.transpose(x, (1, 0, 2, 3)).reshape(KH, T * n, D)

    pack = jnp.concatenate(
        [
            by_head(queries, G),
            by_head(masked, G),
            by_head(response_keys, 1),
            by_head(response_values, 1),
        ],
        axis=1,
    )
    pack = swap_y(pack)
    from_2 = over_z(kv, 2)
    from_m2 = over_z(kv, -2)
    from_1 = over_z(kv, 1)
    from_m1 = over_z(kv, -1)
    from_4 = over_z(from_2, 2)
    from_3 = over_z(from_2, 1)
    from_m3 = over_z(from_m2, -1)

    near = (kv, from_1, from_m1, from_2, from_m2)
    far = (from_3, from_m3, from_4)
    block = jax.ShapeDtypeStruct(kv.shape, bf16)
    spots = kv.shape[2]
    near_keys = 5 * 4 * spots
    far_keys = 3 * 4 * spots
    rows = 4 * R

    def shape(dims, kind):
        return jax.ShapeDtypeStruct(dims, kind)

    def cost(products, keys):
        return products * 2 * rows * keys * D

    weights, acc, top = call(
        functools.partial(near_forward, T=T, G=G),
        "near_forward",
        (
            shape((near_keys + T, rows), bf16),
            shape((D + 16, rows), f32),
            shape((8, rows), f32),
        ),
        [
            pltpu.VMEM((near_keys, D), bf16),
            pltpu.VMEM((near_keys, D), bf16),
            pltpu.VMEM((near_keys + T, R), f32),
            pltpu.VMEM((D + 16, near_keys), bf16),
        ],
        cost(2, near_keys + T),
        pack, *near,
    )
    out, stat, q_near, g_near, dqt, d3, dm3, d4 = call(
        functools.partial(far_both, T=T, G=G),
        "far_both",
        (
            shape((4, R, D), bf16),
            shape((8, rows), f32),
            shape((rows, D), bf16),
            shape((rows, D), bf16),
            shape((D, rows), f32),
            block, block, block,
        ),
        [
            pltpu.VMEM((far_keys, D), bf16),
            pltpu.VMEM((far_keys, D), bf16),
            pltpu.VMEM((far_keys, R), f32),
            pltpu.VMEM((far_keys, rows), bf16),
            pltpu.VMEM((D, far_keys), bf16),
            pltpu.VMEM((D + 16, far_keys), bf16),
            pltpu.VMEM((rows, D), bf16),
            pltpu.VMEM((rows, D), bf16),
        ],
        cost(6, far_keys),
        pack, *far, acc, top,
    )
    home, d0, d1, dm1, d2, dm2 = call(
        functools.partial(near_backward, T=T, G=G),
        "near_backward",
        (shape(pack.shape, bf16), block, block, block, block, block),
        [
            pltpu.VMEM((near_keys, D), bf16),
            pltpu.VMEM((near_keys, D), bf16),
            pltpu.VMEM((D, near_keys), bf16),
            pltpu.VMEM((D, rows), f32),
        ],
        cost(4, near_keys + T),
        pack, *near, weights, out, stat, q_near, g_near, dqt,
    )
    via_2 = over_z(d4, -2)
    via_1 = over_z(d3, -1)
    via_m1 = over_z(dm3, 1)
    (via_2, via_1, via_m1, home, d1, dm1, d2, dm2) = lax.optimization_barrier(
        (via_2, via_1, via_m1, home, d1, dm1, d2, dm2)
    )
    home = swap_y(home)
    far = (d2.astype(f32) + via_1.astype(f32) + via_2.astype(f32)).astype(bf16)
    far_m = (dm2.astype(f32) + via_m1.astype(f32)).astype(bf16)
    parts = [over_z(d1, -1), over_z(dm1, 1), over_z(far, -2), over_z(far_m, 2)]
    total = d0.astype(f32)
    for x in parts:
        total = total + x.astype(f32)
    total = total.astype(bf16)
    total = jnp.stack([total[0]] + [over_y(total[k], -k) for k in (1, 2, 3)])
    total = turned(total, (4 - my_y) % 4)

    def by_token(x, n):
        x = x.reshape(KH, T, n, D)
        return jnp.transpose(x, (1, 0, 2, 3)).reshape(1, T, KH * n, D)

    attended = by_token(home[:, 0:R], G)
    attended = jnp.where(live, attended, jnp.zeros((), bf16))
    return (
        attended,
        by_token(home[:, R:2 * R], G),
        by_token(home[:, 2 * R:2 * R + T], 1),
        by_token(home[:, 2 * R + T:2 * R + 2 * T], 1),
        jnp.transpose(total[:, 0], (1, 0, 2)),
        jnp.transpose(total[:, 1], (1, 0, 2)),
    )


def solution(mesh):
    split = Mesh(mesh.devices.reshape(8, 8, 4), ("batch", "z", "y"))
    spec = P(("batch", "z", "y"))
    return jax.shard_map(
        on_device,
        mesh=split,
        in_specs=(spec,) * 7,
        out_specs=(spec,) * 6,
        check_vma=False,
    )
```

```python
import functools

import jax
import jax.numpy as jnp
from jax import lax
from jax.experimental import pallas as pl
from jax.experimental.pallas import tpu as pltpu
from jax.sharding import Mesh, PartitionSpec as P

LOG2E = 1.4426950408889634
CHUNK = 768
FORWARD_CHUNK = 256
f32 = jnp.float32
bf16 = jnp.bfloat16
NT = (((1,), (1,)), ((), ()))
NN = (((1,), (0,)), ((), ()))
TN = (((0,), (0,)), ((), ()))


def dot(a, b, dims):
    return lax.dot_general(a, b, dims, preferred_element_type=f32)


def sorting(n, token_rows, head_rows):
    per_head = n // 4
    o = lax.broadcasted_iota(jnp.int32, (n, n), 0)
    i = lax.broadcasted_iota(jnp.int32, (n, n), 1)
    head = o // per_head
    rest = o % per_head
    source = (rest // head_rows) * token_rows + head * head_rows + rest % head_rows
    return jnp.where(i == source, 1.0, 0.0).astype(bf16)


def sort_rows(order, x):
    return dot(order, x, NN).astype(bf16)


def unsort_rows(order, x):
    return lax.dot_general(order, x, TN, preferred_element_type=f32).astype(bf16)


def pack_prompt(k_ref, v_ref, out):
    n = k_ref.shape[0]
    order = sorting(n, 4, 1)
    for j, ref in enumerate((k_ref, v_ref)):
        x = sort_rows(order, ref[...])
        for h in range(4):
            out[h, j] = x[h * (n // 4):(h + 1) * (n // 4), :]


def pack_rows(length, q, g, k, v, out, *, T, G):
    R = T * G
    n = 256
    order = sorting(n, 4 * G, G)
    part = n // 4
    row_pos = lax.broadcasted_iota(jnp.int32, (part, 128), 0) // G
    live = length[0]
    for b in range(4 * R // n):
        x = sort_rows(order, q[b * n:(b + 1) * n, :])
        y = sort_rows(order, g[b * n:(b + 1) * n, :])
        alive = row_pos + b * (part // G) < live
        for h in range(4):
            at = slice(b * part, (b + 1) * part)
            out[h, at, :] = x[h * part:(h + 1) * part, :]
            z = y[h * part:(h + 1) * part, :]
            out[h, slice(R + b * part, R + (b + 1) * part), :] = jnp.where(alive, z, jnp.zeros_like(z))
    order = sorting(n, 4, 1)
    for b in range(4 * T // n):
        x = sort_rows(order, k[b * n:(b + 1) * n, :])
        y = sort_rows(order, v[b * n:(b + 1) * n, :])
        for h in range(4):
            at = 2 * R + b * part
            out[h, at:at + part, :] = x[h * part:(h + 1) * part, :]
            out[h, at + T:at + T + part, :] = y[h * part:(h + 1) * part, :]


def unpack_prompt(x, k_out, v_out):
    n = k_out.shape[0]
    order = sorting(n, 4, 1)
    for j, ref in enumerate((k_out, v_out)):
        ref[...] = unsort_rows(order, jnp.concatenate([x[h, j] for h in range(4)], axis=0))


def spans(total, size):
    return [slice(i, min(i + size, total)) for i in range(0, total, size)]


def load_blocks(kvs, K, V, KT, VT):
    spots, D = kvs[0].shape[2], kvs[0].shape[3]
    for i in range(len(kvs)):
        for j in range(4):
            at = (4 * i + j) * spots
            K[at:at + spots, :] = kvs[i][j, 0]
            V[at:at + spots, :] = kvs[i][j, 1]
    for ks in spans(K.shape[0], CHUNK):
        if KT is not None:
            KT[:, ks] = K[ks, :].T
        if VT is not None:
            VT[0:D, ks] = V[ks, :].T
    if VT is not None:
        VT[D:D + 16, :] = jnp.ones((16, K.shape[0]), bf16)


def store_blocks(out_kvs, ks, dk, dv):
    spots = out_kvs[0].shape[2]
    for j in range((ks.stop - ks.start) // spots):
        block = ks.start // spots + j
        part = slice(j * spots, (j + 1) * spots)
        out_kvs[block // 4][block % 4, 0] = dk[part, :].astype(bf16)
        out_kvs[block // 4][block % 4, 1] = dv[part, :].astype(bf16)


def scores_into(S, at, s, top):
    S[at, :] = s
    return jnp.maximum(top, jnp.max(s.reshape(s.shape[0] // 8, 8, s.shape[1]), axis=0))


def near_forward(pack, kv0, kv1, kv2, kv3, kv4, Pm, acc_ref, top_ref, K, V, S, VT, *, T, G):
    D = K.shape[1]
    R = T * G
    C = D ** (-0.5)
    nk = K.shape[0]
    load_blocks((kv0, kv1, kv2, kv3, kv4), K, V, None, VT)
    key_pos = lax.broadcasted_iota(jnp.int32, (T, R), 0)
    row_pos = lax.broadcasted_iota(jnp.int32, (T, R), 1) // G
    own = slice(nk, nk + T)
    parts = spans(nk, FORWARD_CHUNK) + [own]

    def score(r, ks, top):
        qr = pack[r, 0:R, :]
        if ks is own:
            s = dot(pack[r, 2 * R:2 * R + T, :], qr, NT)
            s = jnp.where(key_pos <= row_pos, s, -1e30)
        else:
            s = dot(K[ks, :], qr, NT)
        S[r % 2, ks, :] = s
        return jnp.maximum(top, jnp.max(s.reshape(s.shape[0] // 8, 8, R), axis=0))

    low = jnp.full((8, R), -jnp.inf, f32)
    top = low
    for ks in parts:
        top = score(0, ks, top)
    for r in range(4):
        rows = slice(r * R, (r + 1) * R)
        top = jnp.max(top, axis=0, keepdims=True) * (C * LOG2E)
        top_ref[0:1, rows] = top
        vr = pack[r, 2 * R + T:2 * R + 2 * T, :]
        acc = jnp.zeros((D + 16, R), f32)
        later = low
        for ks in parts:
            if r < 3:
                later = score(r + 1, ks, later)
            p = jnp.exp2(S[r % 2, ks, :] * (C * LOG2E) - top).astype(bf16)
            Pm[ks, rows] = p
            if ks is own:
                acc = acc + dot(jnp.concatenate([vr.T, jnp.ones((16, T), bf16)], axis=0), p, NN)
            else:
                acc = acc + dot(VT[:, ks], p, NN)
        acc_ref[:, rows] = acc
        top = later


def far_both(
    pack, kv0, kv1, kv2, acc_ref, top_ref, o_ref, stat, Qs, Os, dqt, d0, d1, d2,
    K, V, S, Pm, KT, VT, Qn, On, *, T, G
):
    D = K.shape[1]
    R = T * G
    C = D ** (-0.5)
    nk = K.shape[0]
    load_blocks((kv0, kv1, kv2), K, V, KT, VT)
    for r in range(4):
        rows = slice(r * R, (r + 1) * R)
        qr = pack[r, 0:R, :]
        dof = pack[r, R:2 * R, :].astype(f32)
        top = jnp.full((8, R), -jnp.inf, f32)
        for ks in spans(nk, CHUNK):
            top = scores_into(S, ks, dot(K[ks, :], qr, NT), top)
        near_top = top_ref[0:1, rows]
        top = jnp.maximum(near_top, jnp.max(top, axis=0, keepdims=True) * (C * LOG2E))
        near = jnp.exp2(near_top - top)
        acc = acc_ref[:, rows] * near
        for ks in spans(nk, CHUNK):
            p = jnp.exp2(S[ks, :] * (C * LOG2E) - top).astype(bf16)
            Pm[ks, rows] = p
            acc = acc + dot(VT[:, ks], p, NN)
        inv = 1.0 / acc[D:D + 1, :]
        o = (acc[0:D, :] * inv).T.astype(bf16)
        o_ref[r] = o
        delta = jnp.sum(dof * o.astype(f32), axis=1, keepdims=True)
        stat[0:1, rows] = jnp.broadcast_to(delta, (R, D)).T[0:1, :]
        stat[1:2, rows] = inv
        stat[2:3, rows] = inv * near
        inv_col = jnp.broadcast_to(inv, (D, R)).T
        near_col = jnp.broadcast_to(inv * near, (D, R)).T
        qf = qr.astype(f32) * C
        Qn[rows, :] = (qf * inv_col).astype(bf16)
        On[rows, :] = (dof * inv_col).astype(bf16)
        Qs[rows, :] = (qf * near_col).astype(bf16)
        Os[rows, :] = (dof * near_col).astype(bf16)
    for i, ks in enumerate(spans(nk, CHUNK)):
        dk = jnp.zeros((ks.stop - ks.start, D), f32)
        dv = jnp.zeros((ks.stop - ks.start, D), f32)
        for r in range(4):
            rows = slice(r * R, (r + 1) * R)
            p = Pm[ks, rows]
            dp = dot(V[ks, :], pack[r, R:2 * R, :], NT)
            ds = (p.astype(f32) * (dp - stat[0:1, rows])).astype(bf16)
            dk = dk + dot(ds, Qn[rows, :], NN)
            dv = dv + dot(p, On[rows, :], NN)
            part = dot(KT[:, ks], ds, NN) * stat[1:2, rows]
            if i == 0:
                dqt[:, rows] = part
            else:
                dqt[:, rows] += part
        store_blocks((d0, d1, d2), ks, dk, dv)


def near_backward(
    pack, kv0, kv1, kv2, kv3, kv4, Pm, o_ref, stat, Qs, Os, dqt, out, d0, d1, d2, d3, d4,
    K, V, KT, acc, *, T, G
):
    D = K.shape[1]
    R = T * G
    C = D ** (-0.5)
    nk = K.shape[0]
    load_blocks((kv0, kv1, kv2, kv3, kv4), K, V, KT, None)
    own = slice(nk, nk + T)
    for r in range(4):
        rows = slice(r * R, (r + 1) * R)
        kr = pack[r, 2 * R:2 * R + T, :]
        vr = pack[r, 2 * R + T:2 * R + 2 * T, :]
        p = Pm[own, rows]
        ds = (p.astype(f32) * (dot(vr, pack[r, R:2 * R, :], NT) - stat[0:1, rows])).astype(bf16)
        out[r, 0:R, :] = o_ref[r]
        out[r, 2 * R:2 * R + T, :] = dot(ds, Qs[rows, :], NN).astype(bf16)
        out[r, 2 * R + T:2 * R + 2 * T, :] = dot(p, Os[rows, :], NN).astype(bf16)
        acc[:, rows] = dot(kr.T, ds, NN)
    for ks in spans(nk, CHUNK):
        dk = jnp.zeros((ks.stop - ks.start, D), f32)
        dv = jnp.zeros((ks.stop - ks.start, D), f32)
        for r in range(4):
            rows = slice(r * R, (r + 1) * R)
            p = Pm[ks, rows]
            dp = dot(V[ks, :], pack[r, R:2 * R, :], NT)
            ds = (p.astype(f32) * (dp - stat[0:1, rows])).astype(bf16)
            dk = dk + dot(ds, Qs[rows, :], NN)
            dv = dv + dot(p, Os[rows, :], NN)
            acc[:, rows] += dot(KT[:, ks], ds, NN)
        store_blocks((d0, d1, d2, d3, d4), ks, dk, dv)
    for r in range(4):
        rows = slice(r * R, (r + 1) * R)
        dq = (dqt[:, rows] + acc[:, rows] * stat[2:3, rows]) * C
        out[r, R:2 * R, :] = dq.T.astype(bf16)


VMEM_REF = pl.BlockSpec(memory_space=pltpu.VMEM)


def small_call(body, name, out_shape, in_specs, *args):
    return pl.pallas_call(
        body,
        out_shape=out_shape,
        in_specs=in_specs,
        compiler_params=pltpu.CompilerParams(vmem_limit_bytes=16 * 2**20),
        name=name,
    )(*args)


def call(body, name, out_shape, scratch, flops, *args):
    return pl.pallas_call(
        body,
        out_shape=out_shape,
        scratch_shapes=scratch,
        compiler_params=pltpu.CompilerParams(vmem_limit_bytes=32 * 2**20),
        cost_estimate=pl.CostEstimate(flops=flops, bytes_accessed=4 * 2**20, transcendentals=0),
        name=name,
    )(*args)


def on_device(
    queries, response_keys, response_values, prompt_keys, prompt_value_rows, lengths, grad_out
):
    _, T, H, D = queries.shape
    KH = prompt_keys.shape[1]
    G = H // KH
    R = T * G

    def over_z(x, k):
        return lax.ppermute(x, "z", [(i, (i + k) % 8) for i in range(8)])

    def swap_y(x):
        return lax.all_to_all(x, "y", 0, 0, tiled=True)

    spots = prompt_keys.shape[0]

    def flat(x):
        return x.reshape(-1, D)

    kv = small_call(
        pack_prompt,
        "pack_prompt",
        jax.ShapeDtypeStruct((KH, 2, spots, D), bf16),
        [VMEM_REF] * 2,
        flat(prompt_keys), flat(prompt_value_rows),
    )
    kv = swap_y(kv)

    live = (jnp.arange(T) < lengths[0])[:, None, None]
    pack = small_call(
        functools.partial(pack_rows, T=T, G=G),
        "pack_rows",
        jax.ShapeDtypeStruct((KH, 2 * R + 2 * T, D), bf16),
        [pl.BlockSpec(memory_space=pltpu.SMEM)] + [VMEM_REF] * 4,
        lengths, flat(queries), flat(grad_out), flat(response_keys), flat(response_values),
    )
    kv, pack = lax.optimization_barrier((kv, pack))
    pack = swap_y(pack)
    from_2 = over_z(kv, 2)
    from_m2 = over_z(kv, -2)
    from_1 = over_z(kv, 1)
    from_m1 = over_z(kv, -1)
    from_4 = over_z(from_2, 2)
    from_3 = over_z(from_2, 1)
    from_m3 = over_z(from_m2, -1)

    near = (kv, from_1, from_m1, from_2, from_m2)
    far = (from_3, from_m3, from_4)
    block = jax.ShapeDtypeStruct(kv.shape, bf16)
    near_keys = 5 * 4 * spots
    far_keys = 3 * 4 * spots
    rows = 4 * R

    def shape(dims, kind):
        return jax.ShapeDtypeStruct(dims, kind)

    def cost(products, keys):
        return products * 2 * rows * keys * D

    weights, acc, top = call(
        functools.partial(near_forward, T=T, G=G),
        "near_forward",
        (
            shape((near_keys + T, rows), bf16),
            shape((D + 16, rows), f32),
            shape((8, rows), f32),
        ),
        [
            pltpu.VMEM((near_keys, D), bf16),
            pltpu.VMEM((near_keys, D), bf16),
            pltpu.VMEM((2, near_keys + T, R), f32),
            pltpu.VMEM((D + 16, near_keys), bf16),
        ],
        cost(2, near_keys + T),
        pack, *near,
    )
    out, stat, q_near, g_near, dqt, d3, dm3, d4 = call(
        functools.partial(far_both, T=T, G=G),
        "far_both",
        (
            shape((4, R, D), bf16),
            shape((8, rows), f32),
            shape((rows, D), bf16),
            shape((rows, D), bf16),
            shape((D, rows), f32),
            block, block, block,
        ),
        [
            pltpu.VMEM((far_keys, D), bf16),
            pltpu.VMEM((far_keys, D), bf16),
            pltpu.VMEM((far_keys, R), f32),
            pltpu.VMEM((far_keys, rows), bf16),
            pltpu.VMEM((D, far_keys), bf16),
            pltpu.VMEM((D + 16, far_keys), bf16),
            pltpu.VMEM((rows, D), bf16),
            pltpu.VMEM((rows, D), bf16),
        ],
        cost(6, far_keys),
        pack, *far, acc, top,
    )
    home, d0, d1, dm1, d2, dm2 = call(
        functools.partial(near_backward, T=T, G=G),
        "near_backward",
        (shape(pack.shape, bf16), block, block, block, block, block),
        [
            pltpu.VMEM((near_keys, D), bf16),
            pltpu.VMEM((near_keys, D), bf16),
            pltpu.VMEM((D, near_keys), bf16),
            pltpu.VMEM((D, rows), f32),
        ],
        cost(4, near_keys + T),
        pack, *near, weights, out, stat, q_near, g_near, dqt,
    )
    via_2 = over_z(d4, -2)
    via_1 = over_z(d3, -1)
    via_m1 = over_z(dm3, 1)
    (via_2, via_1, via_m1, home, d1, dm1, d2, dm2) = lax.optimization_barrier(
        (via_2, via_1, via_m1, home, d1, dm1, d2, dm2)
    )
    home = swap_y(home)
    far = (d2.astype(f32) + via_1.astype(f32) + via_2.astype(f32)).astype(bf16)
    far_m = (dm2.astype(f32) + via_m1.astype(f32)).astype(bf16)
    parts = [over_z(d1, -1), over_z(dm1, 1), over_z(far, -2), over_z(far_m, 2)]
    total = d0.astype(f32)
    for x in parts:
        total = total + x.astype(f32)
    total, home = lax.optimization_barrier((total.astype(bf16), home))
    total = swap_y(total)

    grad_k, grad_v = small_call(
        unpack_prompt,
        "unpack_prompt",
        (jax.ShapeDtypeStruct((spots * KH, D), bf16),) * 2,
        [VMEM_REF],
        total,
    )

    def by_token(x, n):
        x = x.reshape(KH, T, n, D)
        return jnp.transpose(x, (1, 0, 2, 3)).reshape(1, T, KH * n, D)

    attended = by_token(home[:, 0:R], G)
    attended = jnp.where(live, attended, jnp.zeros((), bf16))
    return (
        attended,
        by_token(home[:, R:2 * R], G),
        by_token(home[:, 2 * R:2 * R + T], 1),
        by_token(home[:, 2 * R + T:2 * R + 2 * T], 1),
        grad_k.reshape(spots, KH, D),
        grad_v.reshape(spots, KH, D),
    )


def solution(mesh):
    split = Mesh(mesh.devices.reshape(8, 8, 4), ("batch", "z", "y"))
    spec = P(("batch", "z", "y"))
    return jax.shard_map(
        on_device,
        mesh=split,
        in_specs=(spec,) * 7,
        out_specs=(spec,) * 6,
        check_vma=False,
    )
```

```python
import functools

import jax
import jax.numpy as jnp
from jax import lax
from jax.experimental import pallas as pl
from jax.experimental.pallas import tpu as pltpu
from jax.sharding import Mesh, PartitionSpec as P

LOG2E = 1.4426950408889634
CHUNK = 768
FORWARD_CHUNK = 256
f32 = jnp.float32
bf16 = jnp.bfloat16
NT = (((1,), (1,)), ((), ()))
NN = (((1,), (0,)), ((), ()))
TN = (((0,), (0,)), ((), ()))


def dot(a, b, dims):
    return lax.dot_general(a, b, dims, preferred_element_type=f32)


def sorting(n, token_rows, head_rows):
    per_head = n // 4
    o = lax.broadcasted_iota(jnp.int32, (n, n), 0)
    i = lax.broadcasted_iota(jnp.int32, (n, n), 1)
    head = o // per_head
    rest = o % per_head
    source = (rest // head_rows) * token_rows + head * head_rows + rest % head_rows
    return jnp.where(i == source, 1.0, 0.0).astype(bf16)


def sort_rows(order, x):
    return dot(order, x, NN).astype(bf16)


def unsort_rows(order, x):
    return lax.dot_general(order, x, TN, preferred_element_type=f32).astype(bf16)


def fetch(refs, held, sems):
    copies = [pltpu.make_async_copy(a, b, sems.at[i]) for i, (a, b) in enumerate(zip(refs, held))]
    for x in copies:
        x.start()
    return copies


def pack_prompt(k_ref, v_ref, out, k_held, v_held, sems):
    copies = fetch((k_ref, v_ref), (k_held, v_held), sems)
    n = k_ref.shape[0]
    order = sorting(n, 4, 1)
    for j, ref in enumerate((k_held, v_held)):
        copies[j].wait()
        x = sort_rows(order, ref[...])
        for h in range(4):
            out[h, j] = x[h * (n // 4):(h + 1) * (n // 4), :]


def pack_rows(length, q_ref, g_ref, k_ref, v_ref, out, q, g, k, v, sems, *, T, G):
    copies = fetch((q_ref, g_ref, k_ref, v_ref), (q, g, k, v), sems)
    R = T * G
    n = 256
    order = sorting(n, 4 * G, G)
    part = n // 4
    row_pos = lax.broadcasted_iota(jnp.int32, (part, 128), 0) // G
    live = length[0]
    copies[0].wait()
    copies[1].wait()
    for b in range(4 * R // n):
        x = sort_rows(order, q[b * n:(b + 1) * n, :])
        y = sort_rows(order, g[b * n:(b + 1) * n, :])
        alive = row_pos + b * (part // G) < live
        for h in range(4):
            at = slice(b * part, (b + 1) * part)
            out[h, at, :] = x[h * part:(h + 1) * part, :]
            z = y[h * part:(h + 1) * part, :]
            out[h, slice(R + b * part, R + (b + 1) * part), :] = jnp.where(alive, z, jnp.zeros_like(z))
    order = sorting(n, 4, 1)
    copies[2].wait()
    copies[3].wait()
    for b in range(4 * T // n):
        x = sort_rows(order, k[b * n:(b + 1) * n, :])
        y = sort_rows(order, v[b * n:(b + 1) * n, :])
        for h in range(4):
            at = 2 * R + b * part
            out[h, at:at + part, :] = x[h * part:(h + 1) * part, :]
            out[h, at + T:at + T + part, :] = y[h * part:(h + 1) * part, :]


def unpack_prompt(x, k_out, v_out):
    n = k_out.shape[0]
    order = sorting(n, 4, 1)
    for j, ref in enumerate((k_out, v_out)):
        ref[...] = unsort_rows(order, jnp.concatenate([x[h, j] for h in range(4)], axis=0))


def spans(total, size):
    return [slice(i, min(i + size, total)) for i in range(0, total, size)]


def load_blocks(kvs, K, V, KT, VT):
    spots, D = kvs[0].shape[2], kvs[0].shape[3]
    for i in range(len(kvs)):
        for j in range(4):
            at = (4 * i + j) * spots
            K[at:at + spots, :] = kvs[i][j, 0]
            V[at:at + spots, :] = kvs[i][j, 1]
    for ks in spans(K.shape[0], CHUNK):
        if KT is not None:
            KT[:, ks] = K[ks, :].T
        if VT is not None:
            VT[0:D, ks] = V[ks, :].T
    if VT is not None:
        VT[D:D + 16, :] = jnp.ones((16, K.shape[0]), bf16)


def store_blocks(out_kvs, ks, dk, dv):
    spots = out_kvs[0].shape[2]
    for j in range((ks.stop - ks.start) // spots):
        block = ks.start // spots + j
        part = slice(j * spots, (j + 1) * spots)
        out_kvs[block // 4][block % 4, 0] = dk[part, :].astype(bf16)
        out_kvs[block // 4][block % 4, 1] = dv[part, :].astype(bf16)


def scores_into(S, at, s, top):
    S[at, :] = s
    return jnp.maximum(top, jnp.max(s.reshape(s.shape[0] // 8, 8, s.shape[1]), axis=0))


def near_forward(pack, kv0, kv1, kv2, kv3, kv4, Pm, acc_ref, top_ref, K, V, S, VT, *, T, G):
    D = K.shape[1]
    R = T * G
    C = D ** (-0.5)
    nk = K.shape[0]
    load_blocks((kv0, kv1, kv2, kv3, kv4), K, V, None, VT)
    key_pos = lax.broadcasted_iota(jnp.int32, (T, R), 0)
    row_pos = lax.broadcasted_iota(jnp.int32, (T, R), 1) // G
    own = slice(nk, nk + T)
    parts = spans(nk, FORWARD_CHUNK) + [own]

    def score(r, ks, top):
        qr = pack[r, 0:R, :]
        if ks is own:
            s = dot(pack[r, 2 * R:2 * R + T, :], qr, NT)
            s = jnp.where(key_pos <= row_pos, s, -1e30)
        else:
            s = dot(K[ks, :], qr, NT)
        S[r % 2, ks, :] = s
        return jnp.maximum(top, jnp.max(s.reshape(s.shape[0] // 8, 8, R), axis=0))

    low = jnp.full((8, R), -jnp.inf, f32)
    top = low
    for ks in parts:
        top = score(0, ks, top)
    for r in range(4):
        rows = slice(r * R, (r + 1) * R)
        top = jnp.max(top, axis=0, keepdims=True) * (C * LOG2E)
        top_ref[0:1, rows] = top
        vr = pack[r, 2 * R + T:2 * R + 2 * T, :]
        acc = jnp.zeros((D + 16, R), f32)
        later = low
        for ks in parts:
            if r < 3:
                later = score(r + 1, ks, later)
            p = jnp.exp2(S[r % 2, ks, :] * (C * LOG2E) - top).astype(bf16)
            Pm[ks, rows] = p
            if ks is own:
                acc = acc + dot(jnp.concatenate([vr.T, jnp.ones((16, T), bf16)], axis=0), p, NN)
            else:
                acc = acc + dot(VT[:, ks], p, NN)
        acc_ref[:, rows] = acc
        top = later


def far_both(
    pack, kv0, kv1, kv2, acc_ref, top_ref, o_ref, stat, Qs, Os, dqt, d0, d1, d2,
    K, V, S, Pm, KT, VT, Qn, On, *, T, G
):
    D = K.shape[1]
    R = T * G
    C = D ** (-0.5)
    nk = K.shape[0]
    load_blocks((kv0, kv1, kv2), K, V, KT, VT)
    for r in range(4):
        rows = slice(r * R, (r + 1) * R)
        qr = pack[r, 0:R, :]
        dof = pack[r, R:2 * R, :].astype(f32)
        top = jnp.full((8, R), -jnp.inf, f32)
        for ks in spans(nk, CHUNK):
            top = scores_into(S, ks, dot(K[ks, :], qr, NT), top)
        near_top = top_ref[0:1, rows]
        top = jnp.maximum(near_top, jnp.max(top, axis=0, keepdims=True) * (C * LOG2E))
        near = jnp.exp2(near_top - top)
        acc = acc_ref[:, rows] * near
        for ks in spans(nk, CHUNK):
            p = jnp.exp2(S[ks, :] * (C * LOG2E) - top).astype(bf16)
            Pm[ks, rows] = p
            acc = acc + dot(VT[:, ks], p, NN)
        inv = 1.0 / acc[D:D + 1, :]
        o = (acc[0:D, :] * inv).T.astype(bf16)
        o_ref[r] = o
        delta = jnp.sum(dof * o.astype(f32), axis=1, keepdims=True)
        stat[0:1, rows] = jnp.broadcast_to(delta, (R, D)).T[0:1, :]
        stat[1:2, rows] = inv
        stat[2:3, rows] = inv * near
        inv_col = jnp.broadcast_to(inv, (D, R)).T
        near_col = jnp.broadcast_to(inv * near, (D, R)).T
        qf = qr.astype(f32) * C
        Qn[rows, :] = (qf * inv_col).astype(bf16)
        On[rows, :] = (dof * inv_col).astype(bf16)
        Qs[rows, :] = (qf * near_col).astype(bf16)
        Os[rows, :] = (dof * near_col).astype(bf16)
    for i, ks in enumerate(spans(nk, CHUNK)):
        dk = jnp.zeros((ks.stop - ks.start, D), f32)
        dv = jnp.zeros((ks.stop - ks.start, D), f32)
        for r in range(4):
            rows = slice(r * R, (r + 1) * R)
            p = Pm[ks, rows]
            dp = dot(V[ks, :], pack[r, R:2 * R, :], NT)
            ds = (p.astype(f32) * (dp - stat[0:1, rows])).astype(bf16)
            dk = dk + dot(ds, Qn[rows, :], NN)
            dv = dv + dot(p, On[rows, :], NN)
            part = dot(KT[:, ks], ds, NN) * stat[1:2, rows]
            if i == 0:
                dqt[:, rows] = part
            else:
                dqt[:, rows] += part
        store_blocks((d0, d1, d2), ks, dk, dv)


def near_backward(
    pack, kv0, kv1, kv2, kv3, kv4, Pm, o_ref, stat, Qs, Os, dqt, out, d0, d1, d2, d3, d4,
    K, V, KT, acc, *, T, G
):
    D = K.shape[1]
    R = T * G
    C = D ** (-0.5)
    nk = K.shape[0]
    load_blocks((kv0, kv1, kv2, kv3, kv4), K, V, KT, None)
    own = slice(nk, nk + T)
    for r in range(4):
        rows = slice(r * R, (r + 1) * R)
        kr = pack[r, 2 * R:2 * R + T, :]
        vr = pack[r, 2 * R + T:2 * R + 2 * T, :]
        p = Pm[own, rows]
        ds = (p.astype(f32) * (dot(vr, pack[r, R:2 * R, :], NT) - stat[0:1, rows])).astype(bf16)
        out[r, 0:R, :] = o_ref[r]
        out[r, 2 * R:2 * R + T, :] = dot(ds, Qs[rows, :], NN).astype(bf16)
        out[r, 2 * R + T:2 * R + 2 * T, :] = dot(p, Os[rows, :], NN).astype(bf16)
        acc[:, rows] = dot(kr.T, ds, NN)
    for ks in spans(nk, CHUNK):
        dk = jnp.zeros((ks.stop - ks.start, D), f32)
        dv = jnp.zeros((ks.stop - ks.start, D), f32)
        for r in range(4):
            rows = slice(r * R, (r + 1) * R)
            p = Pm[ks, rows]
            dp = dot(V[ks, :], pack[r, R:2 * R, :], NT)
            ds = (p.astype(f32) * (dp - stat[0:1, rows])).astype(bf16)
            dk = dk + dot(ds, Qs[rows, :], NN)
            dv = dv + dot(p, Os[rows, :], NN)
            acc[:, rows] += dot(KT[:, ks], ds, NN)
        store_blocks((d0, d1, d2, d3, d4), ks, dk, dv)
    for r in range(4):
        rows = slice(r * R, (r + 1) * R)
        dq = (dqt[:, rows] + acc[:, rows] * stat[2:3, rows]) * C
        out[r, R:2 * R, :] = dq.T.astype(bf16)


VMEM_REF = pl.BlockSpec(memory_space=pltpu.VMEM)
HBM_REF = pl.BlockSpec(memory_space=pltpu.HBM)


def small_call(body, name, out_shape, in_specs, scratch, *args):
    return pl.pallas_call(
        body,
        out_shape=out_shape,
        in_specs=in_specs,
        scratch_shapes=scratch,
        compiler_params=pltpu.CompilerParams(vmem_limit_bytes=16 * 2**20),
        name=name,
    )(*args)


def call(body, name, out_shape, scratch, flops, *args):
    return pl.pallas_call(
        body,
        out_shape=out_shape,
        scratch_shapes=scratch,
        compiler_params=pltpu.CompilerParams(vmem_limit_bytes=32 * 2**20),
        cost_estimate=pl.CostEstimate(flops=flops, bytes_accessed=4 * 2**20, transcendentals=0),
        name=name,
    )(*args)


def on_device(
    queries, response_keys, response_values, prompt_keys, prompt_value_rows, lengths, grad_out
):
    _, T, H, D = queries.shape
    KH = prompt_keys.shape[1]
    G = H // KH
    R = T * G

    def over_z(x, k):
        return lax.ppermute(x, "z", [(i, (i + k) % 8) for i in range(8)])

    def swap_y(x):
        return lax.all_to_all(x, "y", 0, 0, tiled=True)

    spots = prompt_keys.shape[0]

    def flat(x):
        return x.reshape(-1, D)

    kv = small_call(
        pack_prompt,
        "pack_prompt",
        jax.ShapeDtypeStruct((KH, 2, spots, D), bf16),
        [HBM_REF] * 2,
        [pltpu.VMEM((spots * KH, D), bf16)] * 2 + [pltpu.SemaphoreType.DMA((2,))],
        flat(prompt_keys), flat(prompt_value_rows),
    )
    kv = swap_y(kv)

    live = (jnp.arange(T) < lengths[0])[:, None, None]
    pack = small_call(
        functools.partial(pack_rows, T=T, G=G),
        "pack_rows",
        jax.ShapeDtypeStruct((KH, 2 * R + 2 * T, D), bf16),
        [pl.BlockSpec(memory_space=pltpu.SMEM)] + [HBM_REF] * 4,
        [
            pltpu.VMEM((T * H, D), bf16),
            pltpu.VMEM((T * H, D), bf16),
            pltpu.VMEM((T * KH, D), bf16),
            pltpu.VMEM((T * KH, D), bf16),
            pltpu.SemaphoreType.DMA((4,)),
        ],
        lengths, flat(queries), flat(grad_out), flat(response_keys), flat(response_values),
    )
    kv, pack = lax.optimization_barrier((kv, pack))
    pack = swap_y(pack)
    from_2 = over_z(kv, 2)
    from_m2 = over_z(kv, -2)
    from_1 = over_z(kv, 1)
    from_m1 = over_z(kv, -1)
    from_4 = over_z(from_2, 2)
    from_3 = over_z(from_2, 1)
    from_m3 = over_z(from_m2, -1)

    near = (kv, from_1, from_m1, from_2, from_m2)
    far = (from_3, from_m3, from_4)
    block = jax.ShapeDtypeStruct(kv.shape, bf16)
    near_keys = 5 * 4 * spots
    far_keys = 3 * 4 * spots
    rows = 4 * R

    def shape(dims, kind):
        return jax.ShapeDtypeStruct(dims, kind)

    def cost(products, keys):
        return products * 2 * rows * keys * D

    weights, acc, top = call(
        functools.partial(near_forward, T=T, G=G),
        "near_forward",
        (
            shape((near_keys + T, rows), bf16),
            shape((D + 16, rows), f32),
            shape((8, rows), f32),
        ),
        [
            pltpu.VMEM((near_keys, D), bf16),
            pltpu.VMEM((near_keys, D), bf16),
            pltpu.VMEM((2, near_keys + T, R), f32),
            pltpu.VMEM((D + 16, near_keys), bf16),
        ],
        cost(2, near_keys + T),
        pack, *near,
    )
    out, stat, q_near, g_near, dqt, d3, dm3, d4 = call(
        functools.partial(far_both, T=T, G=G),
        "far_both",
        (
            shape((4, R, D), bf16),
            shape((8, rows), f32),
            shape((rows, D), bf16),
            shape((rows, D), bf16),
            shape((D, rows), f32),
            block, block, block,
        ),
        [
            pltpu.VMEM((far_keys, D), bf16),
            pltpu.VMEM((far_keys, D), bf16),
            pltpu.VMEM((far_keys, R), f32),
            pltpu.VMEM((far_keys, rows), bf16),
            pltpu.VMEM((D, far_keys), bf16),
            pltpu.VMEM((D + 16, far_keys), bf16),
            pltpu.VMEM((rows, D), bf16),
            pltpu.VMEM((rows, D), bf16),
        ],
        cost(6, far_keys),
        pack, *far, acc, top,
    )
    home, d0, d1, dm1, d2, dm2 = call(
        functools.partial(near_backward, T=T, G=G),
        "near_backward",
        (shape(pack.shape, bf16), block, block, block, block, block),
        [
            pltpu.VMEM((near_keys, D), bf16),
            pltpu.VMEM((near_keys, D), bf16),
            pltpu.VMEM((D, near_keys), bf16),
            pltpu.VMEM((D, rows), f32),
        ],
        cost(4, near_keys + T),
        pack, *near, weights, out, stat, q_near, g_near, dqt,
    )
    via_2 = over_z(d4, -2)
    via_1 = over_z(d3, -1)
    via_m1 = over_z(dm3, 1)
    (via_2, via_1, via_m1, home, d1, dm1, d2, dm2) = lax.optimization_barrier(
        (via_2, via_1, via_m1, home, d1, dm1, d2, dm2)
    )
    home = swap_y(home)
    far = (d2.astype(f32) + via_1.astype(f32) + via_2.astype(f32)).astype(bf16)
    far_m = (dm2.astype(f32) + via_m1.astype(f32)).astype(bf16)
    parts = [over_z(d1, -1), over_z(dm1, 1), over_z(far, -2), over_z(far_m, 2)]
    total = d0.astype(f32)
    for x in parts:
        total = total + x.astype(f32)
    total, home = lax.optimization_barrier((total.astype(bf16), home))
    total = swap_y(total)

    grad_k, grad_v = small_call(
        unpack_prompt,
        "unpack_prompt",
        (jax.ShapeDtypeStruct((spots * KH, D), bf16),) * 2,
        [VMEM_REF],
        [],
        total,
    )

    def by_token(x, n):
        x = x.reshape(KH, T, n, D)
        return jnp.transpose(x, (1, 0, 2, 3)).reshape(1, T, KH * n, D)

    attended = by_token(home[:, 0:R], G)
    attended = jnp.where(live, attended, jnp.zeros((), bf16))
    return (
        attended,
        by_token(home[:, R:2 * R], G),
        by_token(home[:, 2 * R:2 * R + T], 1),
        by_token(home[:, 2 * R + T:2 * R + 2 * T], 1),
        grad_k.reshape(spots, KH, D),
        grad_v.reshape(spots, KH, D),
    )


def solution(mesh):
    split = Mesh(mesh.devices.reshape(8, 8, 4), ("batch", "z", "y"))
    spec = P(("batch", "z", "y"))
    return jax.shard_map(
        on_device,
        mesh=split,
        in_specs=(spec,) * 7,
        out_specs=(spec,) * 6,
        check_vma=False,
    )
```

```python
import functools

import jax
import jax.numpy as jnp
from jax import lax
from jax.experimental import pallas as pl
from jax.experimental.pallas import tpu as pltpu
from jax.sharding import Mesh, PartitionSpec as P

LOG2E = 1.4426950408889634
CHUNK = 768
FORWARD_CHUNK = 256
FAR_CHUNK = 384
BACKWARD_CHUNK = 512
f32 = jnp.float32
bf16 = jnp.bfloat16
NT = (((1,), (1,)), ((), ()))
NN = (((1,), (0,)), ((), ()))
TN = (((0,), (0,)), ((), ()))


def dot(a, b, dims):
    return lax.dot_general(a, b, dims, preferred_element_type=f32)


def sorting(n, token_rows, head_rows):
    per_head = n // 4
    o = lax.broadcasted_iota(jnp.int32, (n, n), 0)
    i = lax.broadcasted_iota(jnp.int32, (n, n), 1)
    head = o // per_head
    rest = o % per_head
    source = (rest // head_rows) * token_rows + head * head_rows + rest % head_rows
    return jnp.where(i == source, 1.0, 0.0).astype(bf16)


def sort_rows(order, x):
    return dot(order, x, NN).astype(bf16)


def unsort_rows(order, x):
    return lax.dot_general(order, x, TN, preferred_element_type=f32).astype(bf16)


def unpack_prompt(x, k_out, v_out):
    n = k_out.shape[0]
    order = sorting(n, 4, 1)
    for j, ref in enumerate((k_out, v_out)):
        ref[...] = unsort_rows(order, jnp.concatenate([x[h, j] for h in range(4)], axis=0))


def spans(total, size):
    return [slice(i, min(i + size, total)) for i in range(0, total, size)]


def load_blocks(kvs, K, V, KT, VT):
    spots, D = kvs[0].shape[2], kvs[0].shape[3]
    for i in range(len(kvs)):
        for j in range(4):
            at = (4 * i + j) * spots
            K[at:at + spots, :] = kvs[i][j, 0]
            V[at:at + spots, :] = kvs[i][j, 1]
    for ks in spans(K.shape[0], CHUNK):
        if KT is not None:
            KT[:, ks] = K[ks, :].T
        if VT is not None:
            VT[0:D, ks] = V[ks, :].T
    if VT is not None:
        VT[D:D + 16, :] = jnp.ones((16, K.shape[0]), bf16)


def store_blocks(out_kvs, ks, dk, dv):
    spots = out_kvs[0].shape[2]
    for j in range((ks.stop - ks.start) // spots):
        block = ks.start // spots + j
        part = slice(j * spots, (j + 1) * spots)
        out_kvs[block // 4][block % 4, 0] = dk[part, :].astype(bf16)
        out_kvs[block // 4][block % 4, 1] = dv[part, :].astype(bf16)


def scores_into(S, at, s, top):
    S[at, :] = s
    return jnp.maximum(top, jnp.max(s.reshape(s.shape[0] // 8, 8, s.shape[1]), axis=0))


def near_forward(pack, kv0, kv1, kv2, kv3, kv4, Pm, acc_ref, top_ref, K, V, S, VT, *, T, G):
    D = K.shape[1]
    R = T * G
    C = D ** (-0.5)
    nk = K.shape[0]
    load_blocks((kv0, kv1, kv2, kv3, kv4), K, V, None, VT)
    key_pos = lax.broadcasted_iota(jnp.int32, (T, R), 0)
    row_pos = lax.broadcasted_iota(jnp.int32, (T, R), 1) // G
    own = slice(nk, nk + T)
    parts = spans(nk, FORWARD_CHUNK) + [own]

    def score(r, ks, top):
        qr = pack[r, 0:R, :]
        if ks is own:
            s = dot(pack[r, 2 * R:2 * R + T, :], qr, NT)
            s = jnp.where(key_pos <= row_pos, s, -1e30)
        else:
            s = dot(K[ks, :], qr, NT)
        S[r % 2, ks, :] = s
        return jnp.maximum(top, jnp.max(s.reshape(s.shape[0] // 8, 8, R), axis=0))

    low = jnp.full((8, R), -jnp.inf, f32)
    top = low
    for ks in parts:
        top = score(0, ks, top)
    for r in range(4):
        rows = slice(r * R, (r + 1) * R)
        top = jnp.max(top, axis=0, keepdims=True) * (C * LOG2E)
        top_ref[0:1, rows] = top
        vr = pack[r, 2 * R + T:2 * R + 2 * T, :]
        acc = jnp.zeros((D + 16, R), f32)
        later = low
        for ks in parts:
            if r < 3:
                later = score(r + 1, ks, later)
            p = jnp.exp2(S[r % 2, ks, :] * (C * LOG2E) - top).astype(bf16)
            Pm[ks, rows] = p
            if ks is own:
                acc = acc + dot(jnp.concatenate([vr.T, jnp.ones((16, T), bf16)], axis=0), p, NN)
            else:
                acc = acc + dot(VT[:, ks], p, NN)
        acc_ref[:, rows] = acc
        top = later


def far_both(
    pack, kv0, kv1, kv2, acc_ref, top_ref, o_ref, stat, Qs, Os, dqt, d0, d1, d2,
    K, V, S, Pm, KT, VT, Qn, On, *, T, G
):
    D = K.shape[1]
    R = T * G
    C = D ** (-0.5)
    nk = K.shape[0]
    load_blocks((kv0, kv1, kv2), K, V, KT, VT)

    def score(r, ks, top):
        s = dot(K[ks, :], pack[r, 0:R, :], NT)
        S[r % 2, ks, :] = s
        return jnp.maximum(top, jnp.max(s.reshape(s.shape[0] // 8, 8, R), axis=0))

    low = jnp.full((8, R), -jnp.inf, f32)
    later = low
    for ks in spans(nk, FAR_CHUNK):
        later = score(0, ks, later)
    for r in range(4):
        rows = slice(r * R, (r + 1) * R)
        qr = pack[r, 0:R, :]
        dof = pack[r, R:2 * R, :].astype(f32)
        near_top = top_ref[0:1, rows]
        top = jnp.maximum(near_top, jnp.max(later, axis=0, keepdims=True) * (C * LOG2E))
        near = jnp.exp2(near_top - top)
        acc = acc_ref[:, rows] * near
        later = low
        for ks in spans(nk, FAR_CHUNK):
            if r < 3:
                later = score(r + 1, ks, later)
            p = jnp.exp2(S[r % 2, ks, :] * (C * LOG2E) - top).astype(bf16)
            Pm[ks, rows] = p
            acc = acc + dot(VT[:, ks], p, NN)
        inv = 1.0 / acc[D:D + 1, :]
        o = (acc[0:D, :] * inv).T.astype(bf16)
        o_ref[r] = o
        delta = jnp.sum(dof * o.astype(f32), axis=1, keepdims=True)
        stat[0:1, rows] = jnp.broadcast_to(delta, (R, D)).T[0:1, :]
        stat[1:2, rows] = inv
        stat[2:3, rows] = inv * near
        inv_col = jnp.broadcast_to(inv, (D, R)).T
        near_col = jnp.broadcast_to(inv * near, (D, R)).T
        qf = qr.astype(f32) * C
        Qn[rows, :] = (qf * inv_col).astype(bf16)
        On[rows, :] = (dof * inv_col).astype(bf16)
        Qs[rows, :] = (qf * near_col).astype(bf16)
        Os[rows, :] = (dof * near_col).astype(bf16)
    for i, ks in enumerate(spans(nk, CHUNK)):
        dk = jnp.zeros((ks.stop - ks.start, D), f32)
        dv = jnp.zeros((ks.stop - ks.start, D), f32)
        for r in range(4):
            rows = slice(r * R, (r + 1) * R)
            p = Pm[ks, rows]
            dp = dot(V[ks, :], pack[r, R:2 * R, :], NT)
            ds = (p.astype(f32) * (dp - stat[0:1, rows])).astype(bf16)
            dk = dk + dot(ds, Qn[rows, :], NN)
            dv = dv + dot(p, On[rows, :], NN)
            part = dot(KT[:, ks], ds, NN) * stat[1:2, rows]
            if i == 0:
                dqt[:, rows] = part
            else:
                dqt[:, rows] += part
        store_blocks((d0, d1, d2), ks, dk, dv)


def near_backward(
    pack, kv0, kv1, kv2, kv3, kv4, Pm, o_ref, stat, Qs, Os, dqt, out, d0, d1, d2, d3, d4,
    K, V, KT, DS, *, T, G
):
    D = K.shape[1]
    R = T * G
    C = D ** (-0.5)
    nk = K.shape[0]
    load_blocks((kv0, kv1, kv2, kv3, kv4), K, V, KT, None)
    own = slice(nk, nk + T)
    for r in range(4):
        rows = slice(r * R, (r + 1) * R)
        dor = pack[r, R:2 * R, :]
        kr = pack[r, 2 * R:2 * R + T, :]
        vr = pack[r, 2 * R + T:2 * R + 2 * T, :]
        delta = stat[0:1, rows]
        p = Pm[own, rows]
        ds = (p.astype(f32) * (dot(vr, dor, NT) - delta)).astype(bf16)
        out[r, 0:R, :] = o_ref[r]
        out[r, 2 * R:2 * R + T, :] = dot(ds, Qs[rows, :], NN).astype(bf16)
        out[r, 2 * R + T:2 * R + 2 * T, :] = dot(p, Os[rows, :], NN).astype(bf16)
        acc = dot(kr.T, ds, NN)
        for ks in spans(nk, BACKWARD_CHUNK):
            ds = (Pm[ks, rows].astype(f32) * (dot(V[ks, :], dor, NT) - delta)).astype(bf16)
            DS[ks, rows] = ds
        acc = acc + dot(KT[...], DS[:, rows], NN)
        dq = (dqt[:, rows] + acc * stat[2:3, rows]) * C
        out[r, R:2 * R, :] = dq.T.astype(bf16)
    for ks in spans(nk, BACKWARD_CHUNK):
        dk = dot(DS[ks, :], Qs[...], NN)
        dv = dot(Pm[ks, :], Os[...], NN)
        store_blocks((d0, d1, d2, d3, d4), ks, dk, dv)


VMEM_REF = pl.BlockSpec(memory_space=pltpu.VMEM)


def small_call(body, name, out_shape, in_specs, *args):
    return pl.pallas_call(
        body,
        out_shape=out_shape,
        in_specs=in_specs,
        compiler_params=pltpu.CompilerParams(vmem_limit_bytes=16 * 2**20),
        name=name,
    )(*args)


def call(body, name, out_shape, scratch, flops, *args):
    return pl.pallas_call(
        body,
        out_shape=out_shape,
        scratch_shapes=scratch,
        compiler_params=pltpu.CompilerParams(vmem_limit_bytes=32 * 2**20),
        cost_estimate=pl.CostEstimate(flops=flops, bytes_accessed=4 * 2**20, transcendentals=0),
        name=name,
    )(*args)


def on_device(
    queries, response_keys, response_values, prompt_keys, prompt_value_rows, lengths, grad_out
):
    _, T, H, D = queries.shape
    KH = prompt_keys.shape[1]
    G = H // KH
    R = T * G

    def over_z(x, k):
        return lax.ppermute(x, "z", [(i, (i + k) % 8) for i in range(8)])

    def swap_y(x):
        return lax.all_to_all(x, "y", 0, 0, tiled=True)

    kv = jnp.stack([prompt_keys, prompt_value_rows], axis=0)
    kv = swap_y(jnp.transpose(kv, (2, 0, 1, 3)))

    live = (jnp.arange(T) < lengths[0])[:, None, None]
    masked = jnp.where(live, grad_out[0], jnp.zeros((), bf16))

    def by_head(x, n):
        x = x.reshape(T, KH, n, D)
        return jnp.transpose(x, (1, 0, 2, 3)).reshape(KH, T * n, D)

    pack = jnp.concatenate(
        [
            by_head(queries, G),
            by_head(masked, G),
            by_head(response_keys, 1),
            by_head(response_values, 1),
        ],
        axis=1,
    )
    kv, pack = lax.optimization_barrier((kv, pack))
    pack = swap_y(pack)
    from_2 = over_z(kv, 2)
    from_m2 = over_z(kv, -2)
    from_1 = over_z(kv, 1)
    from_m1 = over_z(kv, -1)
    from_4 = over_z(from_2, 2)
    from_3 = over_z(from_2, 1)
    from_m3 = over_z(from_m2, -1)

    near = (kv, from_1, from_m1, from_2, from_m2)
    far = (from_3, from_m3, from_4)
    block = jax.ShapeDtypeStruct(kv.shape, bf16)
    spots = kv.shape[2]
    near_keys = 5 * 4 * spots
    far_keys = 3 * 4 * spots
    rows = 4 * R

    def shape(dims, kind):
        return jax.ShapeDtypeStruct(dims, kind)

    def cost(products, keys):
        return products * 2 * rows * keys * D

    weights, acc, top = call(
        functools.partial(near_forward, T=T, G=G),
        "near_forward",
        (
            shape((near_keys + T, rows), bf16),
            shape((D + 16, rows), f32),
            shape((8, rows), f32),
        ),
        [
            pltpu.VMEM((near_keys, D), bf16),
            pltpu.VMEM((near_keys, D), bf16),
            pltpu.VMEM((2, near_keys + T, R), f32),
            pltpu.VMEM((D + 16, near_keys), bf16),
        ],
        cost(2, near_keys + T),
        pack, *near,
    )
    out, stat, q_near, g_near, dqt, d3, dm3, d4 = call(
        functools.partial(far_both, T=T, G=G),
        "far_both",
        (
            shape((4, R, D), bf16),
            shape((8, rows), f32),
            shape((rows, D), bf16),
            shape((rows, D), bf16),
            shape((D, rows), f32),
            block, block, block,
        ),
        [
            pltpu.VMEM((far_keys, D), bf16),
            pltpu.VMEM((far_keys, D), bf16),
            pltpu.VMEM((2, far_keys, R), f32),
            pltpu.VMEM((far_keys, rows), bf16),
            pltpu.VMEM((D, far_keys), bf16),
            pltpu.VMEM((D + 16, far_keys), bf16),
            pltpu.VMEM((rows, D), bf16),
            pltpu.VMEM((rows, D), bf16),
        ],
        cost(6, far_keys),
        pack, *far, acc, top,
    )
    home, d0, d1, dm1, d2, dm2 = call(
        functools.partial(near_backward, T=T, G=G),
        "near_backward",
        (shape(pack.shape, bf16), block, block, block, block, block),
        [
            pltpu.VMEM((near_keys, D), bf16),
            pltpu.VMEM((near_keys, D), bf16),
            pltpu.VMEM((D, near_keys), bf16),
            pltpu.VMEM((near_keys, rows), bf16),
        ],
        cost(4, near_keys + T),
        pack, *near, weights, out, stat, q_near, g_near, dqt,
    )
    via_2 = over_z(d4, -2)
    via_1 = over_z(d3, -1)
    via_m1 = over_z(dm3, 1)
    (via_2, via_1, via_m1, home, d1, dm1, d2, dm2) = lax.optimization_barrier(
        (via_2, via_1, via_m1, home, d1, dm1, d2, dm2)
    )
    home = swap_y(home)
    far = (d2.astype(f32) + via_1.astype(f32) + via_2.astype(f32)).astype(bf16)
    far_m = (dm2.astype(f32) + via_m1.astype(f32)).astype(bf16)
    parts = [over_z(d1, -1), over_z(dm1, 1), over_z(far, -2), over_z(far_m, 2)]
    total = d0.astype(f32)
    for x in parts:
        total = total + x.astype(f32)
    total, home = lax.optimization_barrier((total.astype(bf16), home))
    total = swap_y(total)

    grad_k, grad_v = small_call(
        unpack_prompt,
        "unpack_prompt",
        (jax.ShapeDtypeStruct((spots * KH, D), bf16),) * 2,
        [VMEM_REF],
        total,
    )

    def by_token(x, n):
        x = x.reshape(KH, T, n, D)
        return jnp.transpose(x, (1, 0, 2, 3)).reshape(1, T, KH * n, D)

    attended = by_token(home[:, 0:R], G)
    attended = jnp.where(live, attended, jnp.zeros((), bf16))
    return (
        attended,
        by_token(home[:, R:2 * R], G),
        by_token(home[:, 2 * R:2 * R + T], 1),
        by_token(home[:, 2 * R + T:2 * R + 2 * T], 1),
        grad_k.reshape(spots, KH, D),
        grad_v.reshape(spots, KH, D),
    )


def solution(mesh):
    split = Mesh(mesh.devices.reshape(8, 8, 4), ("batch", "z", "y"))
    spec = P(("batch", "z", "y"))
    return jax.shard_map(
        on_device,
        mesh=split,
        in_specs=(spec,) * 7,
        out_specs=(spec,) * 6,
        check_vma=False,
    )
```

```python
import functools

import jax
import jax.numpy as jnp
from jax import lax
from jax.experimental import pallas as pl
from jax.experimental.pallas import tpu as pltpu
from jax.sharding import Mesh, PartitionSpec as P

LOG2E = 1.4426950408889634
CHUNK = 768
FORWARD_CHUNK = 256
FAR_CHUNK = 384
BACKWARD_CHUNK = 512
f32 = jnp.float32
bf16 = jnp.bfloat16
NT = (((1,), (1,)), ((), ()))
NN = (((1,), (0,)), ((), ()))
TN = (((0,), (0,)), ((), ()))


def dot(a, b, dims):
    return lax.dot_general(a, b, dims, preferred_element_type=f32)


def sorting(n, token_rows, head_rows):
    per_head = n // 4
    o = lax.broadcasted_iota(jnp.int32, (n, n), 0)
    i = lax.broadcasted_iota(jnp.int32, (n, n), 1)
    head = o // per_head
    rest = o % per_head
    source = (rest // head_rows) * token_rows + head * head_rows + rest % head_rows
    return jnp.where(i == source, 1.0, 0.0).astype(bf16)


def sort_rows(order, x):
    return dot(order, x, NN).astype(bf16)


def unsort_rows(order, x):
    return lax.dot_general(order, x, TN, preferred_element_type=f32).astype(bf16)


def unpack_prompt(x, k_out, v_out):
    n = k_out.shape[0]
    order = sorting(n, 4, 1)
    for j, ref in enumerate((k_out, v_out)):
        ref[...] = unsort_rows(order, jnp.concatenate([x[h, j] for h in range(4)], axis=0))


def spans(total, size):
    return [slice(i, min(i + size, total)) for i in range(0, total, size)]


def load_blocks(kvs, K, V, KT, VT):
    spots, D = kvs[0].shape[2], kvs[0].shape[3]
    for i in range(len(kvs)):
        for j in range(4):
            at = (4 * i + j) * spots
            K[at:at + spots, :] = kvs[i][j, 0]
            V[at:at + spots, :] = kvs[i][j, 1]
    for ks in spans(K.shape[0], CHUNK):
        if KT is not None:
            KT[:, ks] = K[ks, :].T
        if VT is not None:
            VT[0:D, ks] = V[ks, :].T
    if VT is not None:
        VT[D:D + 16, :] = jnp.ones((16, K.shape[0]), bf16)


def store_blocks(places, ks, dk, dv):
    spots = places[0][0].shape[2]
    for j in range((ks.stop - ks.start) // spots):
        out, at = places[ks.start // spots + j]
        part = slice(j * spots, (j + 1) * spots)
        out[at, 0] = dk[part, :].astype(bf16)
        out[at, 1] = dv[part, :].astype(bf16)


def scores_into(S, at, s, top):
    S[at, :] = s
    return jnp.maximum(top, jnp.max(s.reshape(s.shape[0] // 8, 8, s.shape[1]), axis=0))


def near_forward(pack, kv0, kv1, kv2, kv3, kv4, Pm, acc_ref, top_ref, K, V, S, VT, *, T, G):
    D = K.shape[1]
    R = T * G
    C = D ** (-0.5)
    nk = K.shape[0]
    load_blocks((kv0, kv1, kv2, kv3, kv4), K, V, None, VT)
    key_pos = lax.broadcasted_iota(jnp.int32, (T, R), 0)
    row_pos = lax.broadcasted_iota(jnp.int32, (T, R), 1) // G
    own = slice(nk, nk + T)
    parts = spans(nk, FORWARD_CHUNK) + [own]

    def score(r, ks, top):
        qr = pack[r, 0:R, :]
        if ks is own:
            s = dot(pack[r, 2 * R:2 * R + T, :], qr, NT)
            s = jnp.where(key_pos <= row_pos, s, -1e30)
        else:
            s = dot(K[ks, :], qr, NT)
        S[r % 2, ks, :] = s
        return jnp.maximum(top, jnp.max(s.reshape(s.shape[0] // 8, 8, R), axis=0))

    low = jnp.full((8, R), -jnp.inf, f32)
    top = low
    for ks in parts:
        top = score(0, ks, top)
    for r in range(4):
        rows = slice(r * R, (r + 1) * R)
        top = jnp.max(top, axis=0, keepdims=True) * (C * LOG2E)
        top_ref[0:1, rows] = top
        vr = pack[r, 2 * R + T:2 * R + 2 * T, :]
        acc = jnp.zeros((D + 16, R), f32)
        later = low
        for ks in parts:
            if r < 3:
                later = score(r + 1, ks, later)
            p = jnp.exp2(S[r % 2, ks, :] * (C * LOG2E) - top).astype(bf16)
            Pm[ks, rows] = p
            if ks is own:
                acc = acc + dot(jnp.concatenate([vr.T, jnp.ones((16, T), bf16)], axis=0), p, NN)
            else:
                acc = acc + dot(VT[:, ks], p, NN)
        acc_ref[:, rows] = acc
        top = later


def far_both(
    pack, kv0, kv1, kv2, acc_ref, top_ref, o_ref, stat, Qs, Os, dqt, low_out, high_out,
    K, V, S, Pm, KT, VT, Qn, On, *, T, G
):
    D = K.shape[1]
    R = T * G
    C = D ** (-0.5)
    nk = K.shape[0]
    load_blocks((kv0, kv1, kv2), K, V, KT, VT)
    places = [(low_out, i) for i in range(4)] + [(high_out, i) for i in range(4)]
    places += [(low_out, 4), (low_out, 5), (high_out, 4), (high_out, 5)]

    def score(r, ks, top):
        s = dot(K[ks, :], pack[r, 0:R, :], NT)
        S[r % 2, ks, :] = s
        return jnp.maximum(top, jnp.max(s.reshape(s.shape[0] // 8, 8, R), axis=0))

    low = jnp.full((8, R), -jnp.inf, f32)
    later = low
    for ks in spans(nk, FAR_CHUNK):
        later = score(0, ks, later)
    for r in range(4):
        rows = slice(r * R, (r + 1) * R)
        qr = pack[r, 0:R, :]
        dof = pack[r, R:2 * R, :].astype(f32)
        near_top = top_ref[0:1, rows]
        top = jnp.maximum(near_top, jnp.max(later, axis=0, keepdims=True) * (C * LOG2E))
        near = jnp.exp2(near_top - top)
        acc = acc_ref[:, rows] * near
        later = low
        for ks in spans(nk, FAR_CHUNK):
            if r < 3:
                later = score(r + 1, ks, later)
            p = jnp.exp2(S[r % 2, ks, :] * (C * LOG2E) - top).astype(bf16)
            Pm[ks, rows] = p
            acc = acc + dot(VT[:, ks], p, NN)
        inv = 1.0 / acc[D:D + 1, :]
        o = (acc[0:D, :] * inv).T.astype(bf16)
        o_ref[r] = o
        delta = jnp.sum(dof * o.astype(f32), axis=1, keepdims=True)
        stat[0:1, rows] = jnp.broadcast_to(delta, (R, D)).T[0:1, :]
        stat[1:2, rows] = inv
        stat[2:3, rows] = inv * near
        inv_col = jnp.broadcast_to(inv, (D, R)).T
        near_col = jnp.broadcast_to(inv * near, (D, R)).T
        qf = qr.astype(f32) * C
        Qn[rows, :] = (qf * inv_col).astype(bf16)
        On[rows, :] = (dof * inv_col).astype(bf16)
        Qs[rows, :] = (qf * near_col).astype(bf16)
        Os[rows, :] = (dof * near_col).astype(bf16)
    for i, ks in enumerate(spans(nk, CHUNK)):
        dk = jnp.zeros((ks.stop - ks.start, D), f32)
        dv = jnp.zeros((ks.stop - ks.start, D), f32)
        for r in range(4):
            rows = slice(r * R, (r + 1) * R)
            p = Pm[ks, rows]
            dp = dot(V[ks, :], pack[r, R:2 * R, :], NT)
            ds = (p.astype(f32) * (dp - stat[0:1, rows])).astype(bf16)
            dk = dk + dot(ds, Qn[rows, :], NN)
            dv = dv + dot(p, On[rows, :], NN)
            part = dot(KT[:, ks], ds, NN) * stat[1:2, rows]
            if i == 0:
                dqt[:, rows] = part
            else:
                dqt[:, rows] += part
        store_blocks(places, ks, dk, dv)


def near_backward(
    pack, kv0, kv1, kv2, kv3, kv4, Pm, o_ref, stat, Qs, Os, dqt, out, d0, d1, d2, d3, d4,
    K, V, KT, DS, *, T, G
):
    D = K.shape[1]
    R = T * G
    C = D ** (-0.5)
    nk = K.shape[0]
    load_blocks((kv0, kv1, kv2, kv3, kv4), K, V, KT, None)
    places = [(x, i) for x in (d0, d1, d2, d3, d4) for i in range(4)]
    own = slice(nk, nk + T)
    for r in range(4):
        rows = slice(r * R, (r + 1) * R)
        dor = pack[r, R:2 * R, :]
        kr = pack[r, 2 * R:2 * R + T, :]
        vr = pack[r, 2 * R + T:2 * R + 2 * T, :]
        delta = stat[0:1, rows]
        p = Pm[own, rows]
        ds = (p.astype(f32) * (dot(vr, dor, NT) - delta)).astype(bf16)
        out[r, 0:R, :] = o_ref[r]
        out[r, 2 * R:2 * R + T, :] = dot(ds, Qs[rows, :], NN).astype(bf16)
        out[r, 2 * R + T:2 * R + 2 * T, :] = dot(p, Os[rows, :], NN).astype(bf16)
        acc = dot(kr.T, ds, NN)
        for ks in spans(nk, BACKWARD_CHUNK):
            ds = (Pm[ks, rows].astype(f32) * (dot(V[ks, :], dor, NT) - delta)).astype(bf16)
            DS[ks, rows] = ds
        acc = acc + dot(KT[...], DS[:, rows], NN)
        dq = (dqt[:, rows] + acc * stat[2:3, rows]) * C
        out[r, R:2 * R, :] = dq.T.astype(bf16)
    for ks in spans(nk, BACKWARD_CHUNK):
        dk = dot(DS[ks, :], Qs[...], NN)
        dv = dot(Pm[ks, :], Os[...], NN)
        store_blocks(places, ks, dk, dv)


VMEM_REF = pl.BlockSpec(memory_space=pltpu.VMEM)


def small_call(body, name, out_shape, in_specs, *args):
    return pl.pallas_call(
        body,
        out_shape=out_shape,
        in_specs=in_specs,
        compiler_params=pltpu.CompilerParams(vmem_limit_bytes=16 * 2**20),
        name=name,
    )(*args)


def call(body, name, out_shape, scratch, flops, *args):
    return pl.pallas_call(
        body,
        out_shape=out_shape,
        scratch_shapes=scratch,
        compiler_params=pltpu.CompilerParams(vmem_limit_bytes=32 * 2**20),
        cost_estimate=pl.CostEstimate(flops=flops, bytes_accessed=4 * 2**20, transcendentals=0),
        name=name,
    )(*args)


def on_device(
    queries, response_keys, response_values, prompt_keys, prompt_value_rows, lengths, grad_out
):
    _, T, H, D = queries.shape
    KH = prompt_keys.shape[1]
    G = H // KH
    R = T * G

    def over_z(x, k):
        return lax.ppermute(x, "z", [(i, (i + k) % 8) for i in range(8)])

    def swap_y(x):
        return lax.all_to_all(x, "y", 0, 0, tiled=True)

    kv = jnp.stack([prompt_keys, prompt_value_rows], axis=0)
    kv = swap_y(jnp.transpose(kv, (2, 0, 1, 3)))

    live = (jnp.arange(T) < lengths[0])[:, None, None]
    masked = jnp.where(live, grad_out[0], jnp.zeros((), bf16))

    def by_head(x, n):
        x = x.reshape(T, KH, n, D)
        return jnp.transpose(x, (1, 0, 2, 3)).reshape(KH, T * n, D)

    pack = jnp.concatenate(
        [
            by_head(queries, G),
            by_head(masked, G),
            by_head(response_keys, 1),
            by_head(response_values, 1),
        ],
        axis=1,
    )
    kv, pack = lax.optimization_barrier((kv, pack))
    pack = swap_y(pack)
    from_2 = over_z(kv, 2)
    from_m2 = over_z(kv, -2)
    from_1 = over_z(kv, 1)
    from_m1 = over_z(kv, -1)
    from_4 = over_z(from_2, 2)
    from_3 = over_z(from_2, 1)
    from_m3 = over_z(from_m2, -1)

    near = (kv, from_1, from_m1, from_2, from_m2)
    far = (from_3, from_m3, from_4)
    block = jax.ShapeDtypeStruct(kv.shape, bf16)
    spots = kv.shape[2]
    near_keys = 5 * 4 * spots
    far_keys = 3 * 4 * spots
    rows = 4 * R

    def shape(dims, kind):
        return jax.ShapeDtypeStruct(dims, kind)

    def cost(products, keys):
        return products * 2 * rows * keys * D

    weights, acc, top = call(
        functools.partial(near_forward, T=T, G=G),
        "near_forward",
        (
            shape((near_keys + T, rows), bf16),
            shape((D + 16, rows), f32),
            shape((8, rows), f32),
        ),
        [
            pltpu.VMEM((near_keys, D), bf16),
            pltpu.VMEM((near_keys, D), bf16),
            pltpu.VMEM((2, near_keys + T, R), f32),
            pltpu.VMEM((D + 16, near_keys), bf16),
        ],
        cost(2, near_keys + T),
        pack, *near,
    )
    out, stat, q_near, g_near, dqt, down, up = call(
        functools.partial(far_both, T=T, G=G),
        "far_both",
        (
            shape((4, R, D), bf16),
            shape((8, rows), f32),
            shape((rows, D), bf16),
            shape((rows, D), bf16),
            shape((D, rows), f32),
            shape((6,) + kv.shape[1:], bf16),
            shape((6,) + kv.shape[1:], bf16),
        ),
        [
            pltpu.VMEM((far_keys, D), bf16),
            pltpu.VMEM((far_keys, D), bf16),
            pltpu.VMEM((2, far_keys, R), f32),
            pltpu.VMEM((far_keys, rows), bf16),
            pltpu.VMEM((D, far_keys), bf16),
            pltpu.VMEM((D + 16, far_keys), bf16),
            pltpu.VMEM((rows, D), bf16),
            pltpu.VMEM((rows, D), bf16),
        ],
        cost(6, far_keys),
        pack, *far, acc, top,
    )
    home, d0, d1, dm1, d2, dm2 = call(
        functools.partial(near_backward, T=T, G=G),
        "near_backward",
        (shape(pack.shape, bf16), block, block, block, block, block),
        [
            pltpu.VMEM((near_keys, D), bf16),
            pltpu.VMEM((near_keys, D), bf16),
            pltpu.VMEM((D, near_keys), bf16),
            pltpu.VMEM((near_keys, rows), bf16),
        ],
        cost(4, near_keys + T),
        pack, *near, weights, out, stat, q_near, g_near, dqt,
    )
    via_down = over_z(down, -2)
    via_up = over_z(up, 2)
    (via_down, via_up, d1, dm1, d2, dm2) = lax.optimization_barrier(
        (via_down, via_up, d1, dm1, d2, dm2)
    )
    home = swap_y(home)

    def add(x, y):
        return (x.astype(f32) + y.astype(f32)).astype(bf16)

    parts = [
        over_z(jnp.concatenate([add(d2[0:2], via_down[4:6]), d2[2:4]]), -2),
        over_z(jnp.concatenate([dm2[0:2], add(dm2[2:4], via_up[4:6])]), 2),
        over_z(add(d1, via_down[0:4]), -1),
        over_z(add(dm1, via_up[0:4]), 1),
    ]
    total = d0.astype(f32)
    for x in parts:
        total = total + x.astype(f32)
    total, home = lax.optimization_barrier((total.astype(bf16), home))
    total = swap_y(total)

    grad_k, grad_v = small_call(
        unpack_prompt,
        "unpack_prompt",
        (jax.ShapeDtypeStruct((spots * KH, D), bf16),) * 2,
        [VMEM_REF],
        total,
    )

    def by_token(x, n):
        x = x.reshape(KH, T, n, D)
        return jnp.transpose(x, (1, 0, 2, 3)).reshape(1, T, KH * n, D)

    attended = by_token(home[:, 0:R], G)
    attended = jnp.where(live, attended, jnp.zeros((), bf16))
    return (
        attended,
        by_token(home[:, R:2 * R], G),
        by_token(home[:, 2 * R:2 * R + T], 1),
        by_token(home[:, 2 * R + T:2 * R + 2 * T], 1),
        grad_k.reshape(spots, KH, D),
        grad_v.reshape(spots, KH, D),
    )


def solution(mesh):
    split = Mesh(mesh.devices.reshape(8, 8, 4), ("batch", "z", "y"))
    spec = P(("batch", "z", "y"))
    return jax.shard_map(
        on_device,
        mesh=split,
        in_specs=(spec,) * 7,
        out_specs=(spec,) * 6,
        check_vma=False,
    )
```

```python
import functools

import jax
import jax.numpy as jnp
from jax import lax
from jax.experimental import pallas as pl
from jax.experimental.pallas import tpu as pltpu
from jax.sharding import Mesh, PartitionSpec as P

LOG2E = 1.4426950408889634
CHUNK = 768
FORWARD_CHUNK = 256
FAR_CHUNK = 384
BACKWARD_CHUNK = 512
f32 = jnp.float32
bf16 = jnp.bfloat16
NT = (((1,), (1,)), ((), ()))
NN = (((1,), (0,)), ((), ()))
TN = (((0,), (0,)), ((), ()))


def dot(a, b, dims):
    return lax.dot_general(a, b, dims, preferred_element_type=f32)


def sorting(n, token_rows, head_rows):
    per_head = n // 4
    o = lax.broadcasted_iota(jnp.int32, (n, n), 0)
    i = lax.broadcasted_iota(jnp.int32, (n, n), 1)
    head = o // per_head
    rest = o % per_head
    source = (rest // head_rows) * token_rows + head * head_rows + rest % head_rows
    return jnp.where(i == source, 1.0, 0.0).astype(bf16)


def sort_rows(order, x):
    return dot(order, x, NN).astype(bf16)


def unsort_rows(order, x):
    return lax.dot_general(order, x, TN, preferred_element_type=f32).astype(bf16)


def unpack_prompt(x, k_out, v_out):
    n = k_out.shape[0]
    order = sorting(n, 4, 1)
    for j, ref in enumerate((k_out, v_out)):
        ref[...] = unsort_rows(order, jnp.concatenate([x[h, j] for h in range(4)], axis=0))


def spans(total, size):
    return [slice(i, min(i + size, total)) for i in range(0, total, size)]


def load_blocks(kvs, K, V, KT, VT):
    spots, D = kvs[0].shape[2], kvs[0].shape[3]
    for i in range(len(kvs)):
        for j in range(4):
            at = (4 * i + j) * spots
            K[at:at + spots, :] = kvs[i][j, 0]
            V[at:at + spots, :] = kvs[i][j, 1]
    for ks in spans(K.shape[0], CHUNK):
        if KT is not None:
            KT[:, ks] = K[ks, :].T
        if VT is not None:
            VT[0:D, ks] = V[ks, :].T
    if VT is not None:
        VT[D:D + 16, :] = jnp.ones((16, K.shape[0]), bf16)


def store_blocks(places, ks, dk, dv):
    spots = places[0][0].shape[2]
    for j in range((ks.stop - ks.start) // spots):
        out, at = places[ks.start // spots + j]
        part = slice(j * spots, (j + 1) * spots)
        out[at, 0] = dk[part, :].astype(bf16)
        out[at, 1] = dv[part, :].astype(bf16)


def scores_into(S, at, s, top):
    S[at, :] = s
    return jnp.maximum(top, jnp.max(s.reshape(s.shape[0] // 8, 8, s.shape[1]), axis=0))


def near_forward(pack, kv0, kv1, kv2, kv3, kv4, Pm, acc_ref, top_ref, K, V, S, VT, *, T, G):
    D = K.shape[1]
    R = T * G
    C = D ** (-0.5)
    nk = K.shape[0]
    load_blocks((kv0, kv1, kv2, kv3, kv4), K, V, None, VT)
    key_pos = lax.broadcasted_iota(jnp.int32, (T, R), 0)
    row_pos = lax.broadcasted_iota(jnp.int32, (T, R), 1) // G
    own = slice(nk, nk + T)
    parts = spans(nk, FORWARD_CHUNK) + [own]

    def score(r, ks, top):
        qr = pack[r, 0:R, :]
        if ks is own:
            s = dot(pack[r, 2 * R:2 * R + T, :], qr, NT)
            s = jnp.where(key_pos <= row_pos, s, -1e30)
        else:
            s = dot(K[ks, :], qr, NT)
        S[r % 2, ks, :] = s
        return jnp.maximum(top, jnp.max(s.reshape(s.shape[0] // 8, 8, R), axis=0))

    low = jnp.full((8, R), -jnp.inf, f32)
    top = low
    for ks in parts:
        top = score(0, ks, top)
    for r in range(4):
        rows = slice(r * R, (r + 1) * R)
        top = jnp.max(top, axis=0, keepdims=True) * (C * LOG2E)
        top_ref[0:1, rows] = top
        vr = pack[r, 2 * R + T:2 * R + 2 * T, :]
        acc = jnp.zeros((D + 16, R), f32)
        later = low
        for ks in parts:
            if r < 3:
                later = score(r + 1, ks, later)
            p = jnp.exp2(S[r % 2, ks, :] * (C * LOG2E) - top).astype(bf16)
            Pm[ks, rows] = p
            if ks is own:
                acc = acc + dot(jnp.concatenate([vr.T, jnp.ones((16, T), bf16)], axis=0), p, NN)
            else:
                acc = acc + dot(VT[:, ks], p, NN)
        acc_ref[:, rows] = acc
        top = later


def far_both(
    pack, kv0, kv1, kv2, acc_ref, top_ref, o_ref, stat, Qs, Os, dqt, low_out, high_out,
    K, V, S, Pm, KT, VT, Qn, On, *, T, G
):
    D = K.shape[1]
    R = T * G
    C = D ** (-0.5)
    nk = K.shape[0]
    load_blocks((kv0, kv1, kv2), K, V, KT, VT)
    places = [(low_out, i) for i in range(4)] + [(high_out, i) for i in range(4)]
    places += [(low_out, 4), (low_out, 5), (high_out, 4), (high_out, 5)]

    def score(r, ks, top):
        s = dot(K[ks, :], pack[r, 0:R, :], NT)
        S[r % 2, ks, :] = s
        return jnp.maximum(top, jnp.max(s.reshape(s.shape[0] // 8, 8, R), axis=0))

    low = jnp.full((8, R), -jnp.inf, f32)
    later = low
    for ks in spans(nk, FAR_CHUNK):
        later = score(0, ks, later)
    for r in range(4):
        rows = slice(r * R, (r + 1) * R)
        qr = pack[r, 0:R, :]
        dof = pack[r, R:2 * R, :].astype(f32)
        near_top = top_ref[0:1, rows]
        top = jnp.maximum(near_top, jnp.max(later, axis=0, keepdims=True) * (C * LOG2E))
        near = jnp.exp2(near_top - top)
        acc = acc_ref[:, rows] * near
        later = low
        for ks in spans(nk, FAR_CHUNK):
            if r < 3:
                later = score(r + 1, ks, later)
            p = jnp.exp2(S[r % 2, ks, :] * (C * LOG2E) - top).astype(bf16)
            Pm[ks, rows] = p
            acc = acc + dot(VT[:, ks], p, NN)
        inv = 1.0 / acc[D:D + 1, :]
        o = (acc[0:D, :] * inv).T.astype(bf16)
        o_ref[r] = o
        delta = jnp.sum(dof * o.astype(f32), axis=1, keepdims=True)
        stat[0:1, rows] = jnp.broadcast_to(delta, (R, D)).T[0:1, :]
        stat[1:2, rows] = inv
        stat[2:3, rows] = inv * near
        inv_col = jnp.broadcast_to(inv, (D, R)).T
        near_col = jnp.broadcast_to(inv * near, (D, R)).T
        qf = qr.astype(f32) * C
        Qn[rows, :] = (qf * inv_col).astype(bf16)
        On[rows, :] = (dof * inv_col).astype(bf16)
        Qs[rows, :] = (qf * near_col).astype(bf16)
        Os[rows, :] = (dof * near_col).astype(bf16)
    for i, ks in enumerate(spans(nk, CHUNK)):
        dk = jnp.zeros((ks.stop - ks.start, D), f32)
        dv = jnp.zeros((ks.stop - ks.start, D), f32)
        for r in range(4):
            rows = slice(r * R, (r + 1) * R)
            p = Pm[ks, rows]
            dp = dot(V[ks, :], pack[r, R:2 * R, :], NT)
            ds = (p.astype(f32) * (dp - stat[0:1, rows])).astype(bf16)
            dk = dk + dot(ds, Qn[rows, :], NN)
            dv = dv + dot(p, On[rows, :], NN)
            part = dot(KT[:, ks], ds, NN) * stat[1:2, rows]
            if i == 0:
                dqt[:, rows] = part
            else:
                dqt[:, rows] += part
        store_blocks(places, ks, dk, dv)


def near_backward(
    pack, kv0, kv1, kv2, kv3, kv4, Pm, o_ref, stat, Qs, Os, dqt, out, d0, d1, d2, d3, d4,
    K, V, KT, DS, *, T, G
):
    D = K.shape[1]
    R = T * G
    C = D ** (-0.5)
    nk = K.shape[0]
    load_blocks((kv0, kv1, kv2, kv3, kv4), K, V, KT, None)
    places = [(x, i) for x in (d0, d1, d2, d3, d4) for i in range(4)]
    own = slice(nk, nk + T)
    for r in range(4):
        rows = slice(r * R, (r + 1) * R)
        dor = pack[r, R:2 * R, :]
        kr = pack[r, 2 * R:2 * R + T, :]
        vr = pack[r, 2 * R + T:2 * R + 2 * T, :]
        delta = stat[0:1, rows]
        p = Pm[own, rows]
        ds = (p.astype(f32) * (dot(vr, dor, NT) - delta)).astype(bf16)
        out[r, 0:R, :] = o_ref[r]
        out[r, 2 * R:2 * R + T, :] = dot(ds, Qs[rows, :], NN).astype(bf16)
        out[r, 2 * R + T:2 * R + 2 * T, :] = dot(p, Os[rows, :], NN).astype(bf16)
        acc = dot(kr.T, ds, NN)
        for ks in spans(nk, BACKWARD_CHUNK):
            ds = (Pm[ks, rows].astype(f32) * (dot(V[ks, :], dor, NT) - delta)).astype(bf16)
            DS[ks, rows] = ds
        acc = acc + dot(KT[...], DS[:, rows], NN)
        dq = (dqt[:, rows] + acc * stat[2:3, rows]) * C
        out[r, R:2 * R, :] = dq.T.astype(bf16)
    for ks in spans(nk, BACKWARD_CHUNK):
        dk = dot(DS[ks, :], Qs[...], NN)
        dv = dot(Pm[ks, :], Os[...], NN)
        store_blocks(places, ks, dk, dv)


VMEM_REF = pl.BlockSpec(memory_space=pltpu.VMEM)


def small_call(body, name, out_shape, in_specs, *args):
    return pl.pallas_call(
        body,
        out_shape=out_shape,
        in_specs=in_specs,
        compiler_params=pltpu.CompilerParams(vmem_limit_bytes=16 * 2**20),
        name=name,
    )(*args)


def call(body, name, out_shape, scratch, flops, *args):
    return pl.pallas_call(
        body,
        out_shape=out_shape,
        scratch_shapes=scratch,
        compiler_params=pltpu.CompilerParams(vmem_limit_bytes=32 * 2**20),
        cost_estimate=pl.CostEstimate(flops=flops, bytes_accessed=4 * 2**20, transcendentals=0),
        name=name,
    )(*args)


def on_device(
    queries, response_keys, response_values, prompt_keys, prompt_value_rows, lengths, grad_out
):
    _, T, H, D = queries.shape
    KH = prompt_keys.shape[1]
    G = H // KH
    R = T * G

    def over_z(x, k):
        return lax.ppermute(x, "z", [(i, (i + k) % 8) for i in range(8)])

    def swap_y(x):
        return lax.all_to_all(x, "y", 0, 0, tiled=True)

    my_y = lax.axis_index("y")

    def over_y(x, k):
        return lax.ppermute(x, "y", [(i, (i + k) % 4) for i in range(4)])

    def of_head(k):
        h = (my_y + k) % KH
        return jnp.stack(
            [lax.dynamic_index_in_dim(x, h, 1, False) for x in (prompt_keys, prompt_value_rows)]
        )

    kv = jnp.stack([of_head(0)] + [over_y(of_head(4 - m), -m) for m in (1, 2, 3)])

    live = (jnp.arange(T) < lengths[0])[:, None, None]
    masked = jnp.where(live, grad_out[0], jnp.zeros((), bf16))

    def by_head(x, n):
        x = x.reshape(T, KH, n, D)
        return jnp.transpose(x, (1, 0, 2, 3)).reshape(KH, T * n, D)

    pack = jnp.concatenate(
        [
            by_head(queries, G),
            by_head(masked, G),
            by_head(response_keys, 1),
            by_head(response_values, 1),
        ],
        axis=1,
    )
    kv, pack = lax.optimization_barrier((kv, pack))
    pack = swap_y(pack)
    from_2 = over_z(kv, 2)
    from_m2 = over_z(kv, -2)
    from_1 = over_z(kv, 1)
    from_m1 = over_z(kv, -1)
    from_4 = over_z(from_2, 2)
    from_3 = over_z(from_2, 1)
    from_m3 = over_z(from_m2, -1)

    near = (kv, from_1, from_m1, from_2, from_m2)
    far = (from_3, from_m3, from_4)
    block = jax.ShapeDtypeStruct(kv.shape, bf16)
    spots = kv.shape[2]
    near_keys = 5 * 4 * spots
    far_keys = 3 * 4 * spots
    rows = 4 * R

    def shape(dims, kind):
        return jax.ShapeDtypeStruct(dims, kind)

    def cost(products, keys):
        return products * 2 * rows * keys * D

    weights, acc, top = call(
        functools.partial(near_forward, T=T, G=G),
        "near_forward",
        (
            shape((near_keys + T, rows), bf16),
            shape((D + 16, rows), f32),
            shape((8, rows), f32),
        ),
        [
            pltpu.VMEM((near_keys, D), bf16),
            pltpu.VMEM((near_keys, D), bf16),
            pltpu.VMEM((2, near_keys + T, R), f32),
            pltpu.VMEM((D + 16, near_keys), bf16),
        ],
        cost(2, near_keys + T),
        pack, *near,
    )
    out, stat, q_near, g_near, dqt, down, up = call(
        functools.partial(far_both, T=T, G=G),
        "far_both",
        (
            shape((4, R, D), bf16),
            shape((8, rows), f32),
            shape((rows, D), bf16),
            shape((rows, D), bf16),
            shape((D, rows), f32),
            shape((6,) + kv.shape[1:], bf16),
            shape((6,) + kv.shape[1:], bf16),
        ),
        [
            pltpu.VMEM((far_keys, D), bf16),
            pltpu.VMEM((far_keys, D), bf16),
            pltpu.VMEM((2, far_keys, R), f32),
            pltpu.VMEM((far_keys, rows), bf16),
            pltpu.VMEM((D, far_keys), bf16),
            pltpu.VMEM((D + 16, far_keys), bf16),
            pltpu.VMEM((rows, D), bf16),
            pltpu.VMEM((rows, D), bf16),
        ],
        cost(6, far_keys),
        pack, *far, acc, top,
    )
    home, d0, d1, dm1, d2, dm2 = call(
        functools.partial(near_backward, T=T, G=G),
        "near_backward",
        (shape(pack.shape, bf16), block, block, block, block, block),
        [
            pltpu.VMEM((near_keys, D), bf16),
            pltpu.VMEM((near_keys, D), bf16),
            pltpu.VMEM((D, near_keys), bf16),
            pltpu.VMEM((near_keys, rows), bf16),
        ],
        cost(4, near_keys + T),
        pack, *near, weights, out, stat, q_near, g_near, dqt,
    )
    via_down = over_z(down, -2)
    via_up = over_z(up, 2)
    (via_down, via_up, d1, dm1, d2, dm2) = lax.optimization_barrier(
        (via_down, via_up, d1, dm1, d2, dm2)
    )
    home = swap_y(home)

    def add(x, y):
        return (x.astype(f32) + y.astype(f32)).astype(bf16)

    parts = [
        over_z(jnp.concatenate([add(d2[0:2], via_down[4:6]), d2[2:4]]), -2),
        over_z(jnp.concatenate([dm2[0:2], add(dm2[2:4], via_up[4:6])]), 2),
        over_z(add(d1, via_down[0:4]), -1),
        over_z(add(dm1, via_up[0:4]), 1),
    ]
    total = d0.astype(f32)
    for x in parts:
        total = total + x.astype(f32)
    total = total.astype(bf16)
    total = lax.dynamic_slice_in_dim(jnp.concatenate([total, total]), (4 - my_y) % 4, 4, 0)
    total, home = lax.optimization_barrier((total, home))
    total = swap_y(total)

    grad_k, grad_v = small_call(
        unpack_prompt,
        "unpack_prompt",
        (jax.ShapeDtypeStruct((spots * KH, D), bf16),) * 2,
        [VMEM_REF],
        total,
    )

    def by_token(x, n):
        x = x.reshape(KH, T, n, D)
        return jnp.transpose(x, (1, 0, 2, 3)).reshape(1, T, KH * n, D)

    attended = by_token(home[:, 0:R], G)
    attended = jnp.where(live, attended, jnp.zeros((), bf16))
    return (
        attended,
        by_token(home[:, R:2 * R], G),
        by_token(home[:, 2 * R:2 * R + T], 1),
        by_token(home[:, 2 * R + T:2 * R + 2 * T], 1),
        grad_k.reshape(spots, KH, D),
        grad_v.reshape(spots, KH, D),
    )


def solution(mesh):
    split = Mesh(mesh.devices.reshape(8, 8, 4), ("batch", "z", "y"))
    spec = P(("batch", "z", "y"))
    return jax.shard_map(
        on_device,
        mesh=split,
        in_specs=(spec,) * 7,
        out_specs=(spec,) * 6,
        check_vma=False,
    )
```

```python
import functools

import jax
import jax.numpy as jnp
from jax import lax
from jax.experimental import pallas as pl
from jax.experimental.pallas import tpu as pltpu
from jax.sharding import Mesh, PartitionSpec as P

LOG2E = 1.4426950408889634
CHUNK = 768
FORWARD_CHUNK = 256
FAR_CHUNK = 384
BACKWARD_CHUNK = 512
f32 = jnp.float32
bf16 = jnp.bfloat16
NT = (((1,), (1,)), ((), ()))
NN = (((1,), (0,)), ((), ()))
TN = (((0,), (0,)), ((), ()))


def dot(a, b, dims):
    return lax.dot_general(a, b, dims, preferred_element_type=f32)


def sorting(n, token_rows, head_rows):
    per_head = n // 4
    o = lax.broadcasted_iota(jnp.int32, (n, n), 0)
    i = lax.broadcasted_iota(jnp.int32, (n, n), 1)
    head = o // per_head
    rest = o % per_head
    source = (rest // head_rows) * token_rows + head * head_rows + rest % head_rows
    return jnp.where(i == source, 1.0, 0.0).astype(bf16)


def sort_rows(order, x):
    return dot(order, x, NN).astype(bf16)


def unsort_rows(order, x):
    return lax.dot_general(order, x, TN, preferred_element_type=f32).astype(bf16)


def unpack_rows(length, home, o, dq, dk, dv, *, T, G):
    R = T * G
    n = 256
    part = n // 4

    def order(token_rows, head_rows):
        i = lax.broadcasted_iota(jnp.int32, (n, n), 0)
        j = lax.broadcasted_iota(jnp.int32, (n, n), 1)
        in_token = i % token_rows
        block = in_token // head_rows
        source = block * part + (i // token_rows) * head_rows + in_token % head_rows
        return jnp.where(j == source, 1.0, 0.0).astype(bf16)

    def rows(at):
        return jnp.concatenate([home[k, at:at + part, :] for k in range(4)], axis=0)

    by_group = order(4 * G, G)
    token = lax.broadcasted_iota(jnp.int32, (n, 128), 0) // (4 * G)
    live = length[0]
    for b in range(R // part):
        x = sort_rows(by_group, rows(b * part))
        alive = token + b * (n // (4 * G)) < live
        o[b * n:(b + 1) * n, :] = jnp.where(alive, x, jnp.zeros_like(x))
        dq[b * n:(b + 1) * n, :] = sort_rows(by_group, rows(R + b * part))
    by_one = order(4, 1)
    for b in range(T // part):
        dk[b * n:(b + 1) * n, :] = sort_rows(by_one, rows(2 * R + b * part))
        dv[b * n:(b + 1) * n, :] = sort_rows(by_one, rows(2 * R + T + b * part))


def unpack_prompt(place, b0, b1, b2, b3, k_out, v_out):
    n = k_out.shape[0]
    i = lax.broadcasted_iota(jnp.int32, (n, n), 0)
    j = lax.broadcasted_iota(jnp.int32, (n, n), 1)
    source = ((place[0] + 4 - i % 4) % 4) * (n // 4) + i // 4
    order = jnp.where(j == source, 1.0, 0.0).astype(bf16)
    for which, ref in enumerate((k_out, v_out)):
        x = jnp.concatenate([x[which] for x in (b0, b1, b2, b3)], axis=0)
        ref[...] = sort_rows(order, x)


def spans(total, size):
    return [slice(i, min(i + size, total)) for i in range(0, total, size)]


def load_blocks(kvs, K, V, KT, VT):
    spots, D = kvs[0].shape[2], kvs[0].shape[3]
    for i in range(len(kvs)):
        for j in range(4):
            at = (4 * i + j) * spots
            K[at:at + spots, :] = kvs[i][j, 0]
            V[at:at + spots, :] = kvs[i][j, 1]
    for ks in spans(K.shape[0], CHUNK):
        if KT is not None:
            KT[:, ks] = K[ks, :].T
        if VT is not None:
            VT[0:D, ks] = V[ks, :].T
    if VT is not None:
        VT[D:D + 16, :] = jnp.ones((16, K.shape[0]), bf16)


def store_blocks(places, ks, dk, dv):
    spots = places[0][0].shape[2]
    for j in range((ks.stop - ks.start) // spots):
        out, at = places[ks.start // spots + j]
        part = slice(j * spots, (j + 1) * spots)
        out[at, 0] = dk[part, :].astype(bf16)
        out[at, 1] = dv[part, :].astype(bf16)


def scores_into(S, at, s, top):
    S[at, :] = s
    return jnp.maximum(top, jnp.max(s.reshape(s.shape[0] // 8, 8, s.shape[1]), axis=0))


def near_forward(pack, kv0, kv1, kv2, kv3, kv4, Pm, acc_ref, top_ref, K, V, S, VT, *, T, G):
    D = K.shape[1]
    R = T * G
    C = D ** (-0.5)
    nk = K.shape[0]
    load_blocks((kv0, kv1, kv2, kv3, kv4), K, V, None, VT)
    key_pos = lax.broadcasted_iota(jnp.int32, (T, R), 0)
    row_pos = lax.broadcasted_iota(jnp.int32, (T, R), 1) // G
    own = slice(nk, nk + T)
    parts = spans(nk, FORWARD_CHUNK) + [own]

    def score(r, ks, top):
        qr = pack[r, 0:R, :]
        if ks is own:
            s = dot(pack[r, 2 * R:2 * R + T, :], qr, NT)
            s = jnp.where(key_pos <= row_pos, s, -1e30)
        else:
            s = dot(K[ks, :], qr, NT)
        S[r % 2, ks, :] = s
        return jnp.maximum(top, jnp.max(s.reshape(s.shape[0] // 8, 8, R), axis=0))

    low = jnp.full((8, R), -jnp.inf, f32)
    top = low
    for ks in parts:
        top = score(0, ks, top)
    for r in range(4):
        rows = slice(r * R, (r + 1) * R)
        top = jnp.max(top, axis=0, keepdims=True) * (C * LOG2E)
        top_ref[0:1, rows] = top
        vr = pack[r, 2 * R + T:2 * R + 2 * T, :]
        acc = jnp.zeros((D + 16, R), f32)
        later = low
        for ks in parts:
            if r < 3:
                later = score(r + 1, ks, later)
            p = jnp.exp2(S[r % 2, ks, :] * (C * LOG2E) - top).astype(bf16)
            Pm[ks, rows] = p
            if ks is own:
                acc = acc + dot(jnp.concatenate([vr.T, jnp.ones((16, T), bf16)], axis=0), p, NN)
            else:
                acc = acc + dot(VT[:, ks], p, NN)
        acc_ref[:, rows] = acc
        top = later


def far_both(
    pack, kv0, kv1, kv2, acc_ref, top_ref, o_ref, stat, Qs, Os, dqt, low_out, high_out,
    K, V, S, Pm, KT, VT, Qn, On, *, T, G
):
    D = K.shape[1]
    R = T * G
    C = D ** (-0.5)
    nk = K.shape[0]
    load_blocks((kv0, kv1, kv2), K, V, KT, VT)
    places = [(low_out, i) for i in range(4)] + [(high_out, i) for i in range(4)]
    places += [(low_out, 4), (low_out, 5), (high_out, 4), (high_out, 5)]

    def score(r, ks, top):
        s = dot(K[ks, :], pack[r, 0:R, :], NT)
        S[r % 2, ks, :] = s
        return jnp.maximum(top, jnp.max(s.reshape(s.shape[0] // 8, 8, R), axis=0))

    low = jnp.full((8, R), -jnp.inf, f32)
    later = low
    for ks in spans(nk, FAR_CHUNK):
        later = score(0, ks, later)
    for r in range(4):
        rows = slice(r * R, (r + 1) * R)
        qr = pack[r, 0:R, :]
        dof = pack[r, R:2 * R, :].astype(f32)
        near_top = top_ref[0:1, rows]
        top = jnp.maximum(near_top, jnp.max(later, axis=0, keepdims=True) * (C * LOG2E))
        near = jnp.exp2(near_top - top)
        acc = acc_ref[:, rows] * near
        later = low
        for ks in spans(nk, FAR_CHUNK):
            if r < 3:
                later = score(r + 1, ks, later)
            p = jnp.exp2(S[r % 2, ks, :] * (C * LOG2E) - top).astype(bf16)
            Pm[ks, rows] = p
            acc = acc + dot(VT[:, ks], p, NN)
        inv = 1.0 / acc[D:D + 1, :]
        o = (acc[0:D, :] * inv).T.astype(bf16)
        o_ref[r] = o
        delta = jnp.sum(dof * o.astype(f32), axis=1, keepdims=True)
        stat[0:1, rows] = jnp.broadcast_to(delta, (R, D)).T[0:1, :]
        stat[1:2, rows] = inv
        stat[2:3, rows] = inv * near
        inv_col = jnp.broadcast_to(inv, (D, R)).T
        near_col = jnp.broadcast_to(inv * near, (D, R)).T
        qf = qr.astype(f32) * C
        Qn[rows, :] = (qf * inv_col).astype(bf16)
        On[rows, :] = (dof * inv_col).astype(bf16)
        Qs[rows, :] = (qf * near_col).astype(bf16)
        Os[rows, :] = (dof * near_col).astype(bf16)
    for i, ks in enumerate(spans(nk, CHUNK)):
        dk = jnp.zeros((ks.stop - ks.start, D), f32)
        dv = jnp.zeros((ks.stop - ks.start, D), f32)
        for r in range(4):
            rows = slice(r * R, (r + 1) * R)
            p = Pm[ks, rows]
            dp = dot(V[ks, :], pack[r, R:2 * R, :], NT)
            ds = (p.astype(f32) * (dp - stat[0:1, rows])).astype(bf16)
            dk = dk + dot(ds, Qn[rows, :], NN)
            dv = dv + dot(p, On[rows, :], NN)
            part = dot(KT[:, ks], ds, NN) * stat[1:2, rows]
            if i == 0:
                dqt[:, rows] = part
            else:
                dqt[:, rows] += part
        store_blocks(places, ks, dk, dv)


def near_backward(
    pack, kv0, kv1, kv2, kv3, kv4, Pm, o_ref, stat, Qs, Os, dqt, out, d0, d1, d2, d3, d4,
    K, V, KT, DS, *, T, G
):
    D = K.shape[1]
    R = T * G
    C = D ** (-0.5)
    nk = K.shape[0]
    load_blocks((kv0, kv1, kv2, kv3, kv4), K, V, KT, None)
    places = [(x, i) for x in (d0, d1, d2, d3, d4) for i in range(4)]
    own = slice(nk, nk + T)
    for r in range(4):
        rows = slice(r * R, (r + 1) * R)
        dor = pack[r, R:2 * R, :]
        kr = pack[r, 2 * R:2 * R + T, :]
        vr = pack[r, 2 * R + T:2 * R + 2 * T, :]
        delta = stat[0:1, rows]
        p = Pm[own, rows]
        ds = (p.astype(f32) * (dot(vr, dor, NT) - delta)).astype(bf16)
        out[r, 0:R, :] = o_ref[r]
        out[r, 2 * R:2 * R + T, :] = dot(ds, Qs[rows, :], NN).astype(bf16)
        out[r, 2 * R + T:2 * R + 2 * T, :] = dot(p, Os[rows, :], NN).astype(bf16)
        acc = dot(kr.T, ds, NN)
        for ks in spans(nk, BACKWARD_CHUNK):
            ds = (Pm[ks, rows].astype(f32) * (dot(V[ks, :], dor, NT) - delta)).astype(bf16)
            DS[ks, rows] = ds
        acc = acc + dot(KT[...], DS[:, rows], NN)
        dq = (dqt[:, rows] + acc * stat[2:3, rows]) * C
        out[r, R:2 * R, :] = dq.T.astype(bf16)
    for ks in spans(nk, BACKWARD_CHUNK):
        dk = dot(DS[ks, :], Qs[...], NN)
        dv = dot(Pm[ks, :], Os[...], NN)
        store_blocks(places, ks, dk, dv)


VMEM_REF = pl.BlockSpec(memory_space=pltpu.VMEM)


def small_call(body, name, out_shape, in_specs, *args):
    return pl.pallas_call(
        body,
        out_shape=out_shape,
        in_specs=in_specs,
        compiler_params=pltpu.CompilerParams(vmem_limit_bytes=16 * 2**20),
        name=name,
    )(*args)


def call(body, name, out_shape, scratch, flops, *args):
    return pl.pallas_call(
        body,
        out_shape=out_shape,
        scratch_shapes=scratch,
        compiler_params=pltpu.CompilerParams(vmem_limit_bytes=32 * 2**20),
        cost_estimate=pl.CostEstimate(flops=flops, bytes_accessed=4 * 2**20, transcendentals=0),
        name=name,
    )(*args)


def on_device(
    queries, response_keys, response_values, prompt_keys, prompt_value_rows, lengths, grad_out
):
    _, T, H, D = queries.shape
    KH = prompt_keys.shape[1]
    G = H // KH
    R = T * G

    def over_z(x, k):
        return lax.ppermute(x, "z", [(i, (i + k) % 8) for i in range(8)])

    def swap_y(x):
        return lax.all_to_all(x, "y", 0, 0, tiled=True)

    my_y = lax.axis_index("y")

    def over_y(x, k):
        return lax.ppermute(x, "y", [(i, (i + k) % 4) for i in range(4)])

    def of_head(k):
        h = (my_y + k) % KH
        return jnp.stack(
            [lax.dynamic_index_in_dim(x, h, 1, False) for x in (prompt_keys, prompt_value_rows)]
        )

    kv = jnp.stack([of_head(0)] + [over_y(of_head(4 - m), -m) for m in (1, 2, 3)])

    live = (jnp.arange(T) < lengths[0])[:, None, None]
    masked = jnp.where(live, grad_out[0], jnp.zeros((), bf16))

    def by_head(x, n):
        x = x.reshape(T, KH, n, D)
        return jnp.transpose(x, (1, 0, 2, 3)).reshape(KH, T * n, D)

    pack = jnp.concatenate(
        [
            by_head(queries, G),
            by_head(masked, G),
            by_head(response_keys, 1),
            by_head(response_values, 1),
        ],
        axis=1,
    )
    kv, pack = lax.optimization_barrier((kv, pack))
    pack = swap_y(pack)
    from_2 = over_z(kv, 2)
    from_m2 = over_z(kv, -2)
    from_1 = over_z(kv, 1)
    from_m1 = over_z(kv, -1)
    from_4 = over_z(from_2, 2)
    from_3 = over_z(from_2, 1)
    from_m3 = over_z(from_m2, -1)

    near = (kv, from_1, from_m1, from_2, from_m2)
    far = (from_3, from_m3, from_4)
    block = jax.ShapeDtypeStruct(kv.shape, bf16)
    spots = kv.shape[2]
    near_keys = 5 * 4 * spots
    far_keys = 3 * 4 * spots
    rows = 4 * R

    def shape(dims, kind):
        return jax.ShapeDtypeStruct(dims, kind)

    def cost(products, keys):
        return products * 2 * rows * keys * D

    weights, acc, top = call(
        functools.partial(near_forward, T=T, G=G),
        "near_forward",
        (
            shape((near_keys + T, rows), bf16),
            shape((D + 16, rows), f32),
            shape((8, rows), f32),
        ),
        [
            pltpu.VMEM((near_keys, D), bf16),
            pltpu.VMEM((near_keys, D), bf16),
            pltpu.VMEM((2, near_keys + T, R), f32),
            pltpu.VMEM((D + 16, near_keys), bf16),
        ],
        cost(2, near_keys + T),
        pack, *near,
    )
    out, stat, q_near, g_near, dqt, down, up = call(
        functools.partial(far_both, T=T, G=G),
        "far_both",
        (
            shape((4, R, D), bf16),
            shape((8, rows), f32),
            shape((rows, D), bf16),
            shape((rows, D), bf16),
            shape((D, rows), f32),
            shape((6,) + kv.shape[1:], bf16),
            shape((6,) + kv.shape[1:], bf16),
        ),
        [
            pltpu.VMEM((far_keys, D), bf16),
            pltpu.VMEM((far_keys, D), bf16),
            pltpu.VMEM((2, far_keys, R), f32),
            pltpu.VMEM((far_keys, rows), bf16),
            pltpu.VMEM((D, far_keys), bf16),
            pltpu.VMEM((D + 16, far_keys), bf16),
            pltpu.VMEM((rows, D), bf16),
            pltpu.VMEM((rows, D), bf16),
        ],
        cost(6, far_keys),
        pack, *far, acc, top,
    )
    home, d0, d1, dm1, d2, dm2 = call(
        functools.partial(near_backward, T=T, G=G),
        "near_backward",
        (shape(pack.shape, bf16), block, block, block, block, block),
        [
            pltpu.VMEM((near_keys, D), bf16),
            pltpu.VMEM((near_keys, D), bf16),
            pltpu.VMEM((D, near_keys), bf16),
            pltpu.VMEM((near_keys, rows), bf16),
        ],
        cost(4, near_keys + T),
        pack, *near, weights, out, stat, q_near, g_near, dqt,
    )
    via_down = over_z(down, -2)
    via_up = over_z(up, 2)
    (via_down, via_up, d1, dm1, d2, dm2) = lax.optimization_barrier(
        (via_down, via_up, d1, dm1, d2, dm2)
    )
    home = swap_y(home)

    def add(x, y):
        return (x.astype(f32) + y.astype(f32)).astype(bf16)

    parts = [
        over_z(jnp.concatenate([add(d2[0:2], via_down[4:6]), d2[2:4]]), -2),
        over_z(jnp.concatenate([dm2[0:2], add(dm2[2:4], via_up[4:6])]), 2),
        over_z(add(d1, via_down[0:4]), -1),
        over_z(add(dm1, via_up[0:4]), 1),
    ]
    total = d0.astype(f32)
    for x in parts:
        total = total + x.astype(f32)
    total = total.astype(bf16)
    total, home = lax.optimization_barrier((total, home))
    blocks = [total[0]] + [over_y(total[m], m) for m in (1, 2, 3)]
    blocks[1], home = lax.optimization_barrier((blocks[1], home))

    grad_k, grad_v = small_call(
        unpack_prompt,
        "unpack_prompt",
        (jax.ShapeDtypeStruct((spots * KH, D), bf16),) * 2,
        [pl.BlockSpec(memory_space=pltpu.SMEM)] + [VMEM_REF] * 4,
        my_y.astype(jnp.int32)[None], *blocks,
    )

    attended, grad_query, grad_rk, grad_rv = small_call(
        functools.partial(unpack_rows, T=T, G=G),
        "unpack_rows",
        (jax.ShapeDtypeStruct((T * H, D), bf16),) * 2
        + (jax.ShapeDtypeStruct((T * KH, D), bf16),) * 2,
        [pl.BlockSpec(memory_space=pltpu.SMEM), VMEM_REF],
        lengths, home,
    )
    return (
        attended.reshape(1, T, H, D),
        grad_query.reshape(1, T, H, D),
        grad_rk.reshape(1, T, KH, D),
        grad_rv.reshape(1, T, KH, D),
        grad_k.reshape(spots, KH, D),
        grad_v.reshape(spots, KH, D),
    )


def solution(mesh):
    split = Mesh(mesh.devices.reshape(8, 8, 4), ("batch", "z", "y"))
    spec = P(("batch", "z", "y"))
    return jax.shard_map(
        on_device,
        mesh=split,
        in_specs=(spec,) * 7,
        out_specs=(spec,) * 6,
        check_vma=False,
    )
```
